256 devices in a mesh: lat: 16 (over y, x_lo, core), lon: 16 (over z, x_hi).
Axes of the slice: x: 4 (x_hi: 2, x_lo: 2; x = x_hi * 2 + x_lo), y: 4, z: 8, core: 2. Of those that a mesh axis runs over, the one named last changes fastest.
Arguments:
- tokens: bfloat16 [2, 96, 192, 512], P(None, 'lat', 'lon'), may hold values from -6 to 6
- labels: int32 [2, 96, 192], P(None, 'lat', 'lon'), may hold values from 0 to 2
- gain_one: float32 [512], replicated, may hold values from 0.25 to 1.75
- project_one: bfloat16 [512, 1536], replicated, may hold values from -0.25 to 0.25
- output_one: bfloat16 [512, 512], replicated, may hold values from -0.25 to 0.25
- bias_one: bfloat16 [16, 144, 144], replicated, may hold values from -4 to 4
- gain_two: float32 [512], replicated, may hold values from 0.25 to 1.75
- project_two: bfloat16 [512, 1536], replicated, may hold values from -0.25 to 0.25
- output_two: bfloat16 [512, 512], replicated, may hold values from -0.25 to 0.25
- bias_two: bfloat16 [16, 144, 144], replicated, may hold values from -4 to 4
- gain_three: float32 [512], replicated, may hold values from 0.25 to 1.75
- up_weight: bfloat16 [512, 2048], replicated, may hold values from -0.25 to 0.25
- down_weight: bfloat16 [2048, 512], replicated, may hold values from -0.125 to 0.125
- cotangent: bfloat16 [2, 96, 192, 512], P(None, 'lat', 'lon'), may hold values from -6 to 6
Outputs:
- outputs: bfloat16 [2, 96, 192, 512], P(None, 'lat', 'lon')
- input_grad: bfloat16 [2, 96, 192, 512], P(None, 'lat', 'lon')
The draws below stay inside these ranges and needn't reach their ends.
All inputs are finite; a program needn't handle non-finite values.
Results may differ from the reference program's by a relative error of at most 0.028.
Values may be sent and summed in bfloat16 or wider, within the bound.
A program may use at most 128 MiB of HBM per device.

```python
import jax
import jax.numpy as jnp
from jax import lax

D = 512
HEADS = 16
FF = 2048
LEV = 2
WLAT = 6
WLON = 12
WT = 144
NLAT = 96
NLON = 192


def place_ends(drawn, rng, least, largest):
    place = [jax.random.randint(jax.random.fold_in(rng, axis), (), 0, length) for axis, length in enumerate(drawn.shape)]
    longest = drawn.shape.index(max(drawn.shape))
    next_to = place[:longest] + [(place[longest] + 1) % drawn.shape[longest]] + place[longest + 1:]
    return drawn.at[tuple(place)].set(least).at[tuple(next_to)].set(largest)


def block_levels(key, extent, cuts, smallest, top_value):
    level = 1.0
    for dim, blocks in cuts:
        draws = jax.random.uniform(jax.random.fold_in(jax.random.fold_in(key, 6), dim), (blocks,), jnp.float32, smallest / len(cuts), top_value / len(cuts))
        level = level * jnp.repeat(jnp.exp(draws), extent[dim] // blocks).reshape((-1,) + (1,) * (len(extent) - 1 - dim))
    return level


def noise(rng, shape, width, most, cuts=(), kind=jnp.bfloat16):
    entries = jax.random.normal(rng, shape, jnp.float32) * width
    if len(cuts) > 0:
        entries = block_levels(rng, shape, cuts, -0.22, 0.18) * entries
    return jnp.clip(entries, min=-most, max=most).astype(kind)


def setup_inputs(seed: int = 0) -> dict:
    seeds = jax.random.split(jax.random.key(seed), 15)
    return {
        "tokens": noise(seeds[0], (LEV, NLAT, NLON, D), 1.0, 6.0, ((1, 16), (2, 16))),
        "labels": place_ends(jax.random.randint(seeds[1], (LEV, NLAT, NLON), 0, 3), jax.random.fold_in(seeds[1], 1), 0, 2).astype(jnp.int32),
        "gain_one": jnp.clip(1.0 + 0.15 * jax.random.normal(seeds[2], (D,), jnp.float32), 0.25, 1.75),
        "project_one": noise(seeds[3], (D, 3 * D), D ** -0.5, 0.25),
        "output_one": noise(seeds[4], (D, D), D ** -0.5, 0.25),
        "bias_one": noise(seeds[5], (HEADS, WT, WT), 1.0, 4.0),
        "gain_two": jnp.clip(1.0 + 0.15 * jax.random.normal(seeds[6], (D,), jnp.float32), 0.25, 1.75),
        "project_two": noise(seeds[7], (D, 3 * D), D ** -0.5, 0.25),
        "output_two": noise(seeds[8], (D, D), D ** -0.5, 0.25),
        "bias_two": noise(seeds[9], (HEADS, WT, WT), 1.0, 4.0),
        "gain_three": jnp.clip(1.0 + 0.15 * jax.random.normal(seeds[10], (D,), jnp.float32), 0.25, 1.75),
        "up_weight": noise(seeds[11], (D, FF), D ** -0.5, 0.25),
        "down_weight": noise(seeds[12], (FF, D), FF ** -0.5, 0.125),
        "cotangent": noise(seeds[13], (LEV, NLAT, NLON, D), 1.0, 6.0, ((1, 16), (2, 16))),
    }


EPSILON = 1e-05

def normalize(field_in, gain_vec):
    average = lax.optimization_barrier(jnp.mean(field_in, axis=-1, keepdims=True))
    centred = field_in - average
    variance = lax.optimization_barrier(jnp.mean(centred * centred, axis=-1, keepdims=True))
    return (centred * lax.rsqrt(variance + EPSILON) * gain_vec).astype(jnp.bfloat16)

def to_windows(grid_in, win_lat, win_lon):
    levels, lat_rows, lon_cols = (grid_in.shape[0], grid_in.shape[1], grid_in.shape[2])
    trailing = grid_in.shape[3:]
    parted = grid_in.reshape((levels, lat_rows // win_lat, win_lat, lon_cols // win_lon, win_lon) + trailing)
    permute = (1, 3, 0, 2, 4) + tuple(range(5, 5 + len(trailing)))
    return parted.transpose(permute).reshape((lat_rows // win_lat * (lon_cols // win_lon), levels * win_lat * win_lon) + trailing)

def from_windows(blocks, levels, lat_rows, lon_cols, win_lat, win_lon):
    trailing = blocks.shape[2:]
    parted = blocks.reshape((lat_rows // win_lat, lon_cols // win_lon, levels, win_lat, win_lon) + trailing)
    permute = (2, 0, 3, 1, 4) + tuple(range(5, 5 + len(trailing)))
    return parted.transpose(permute).reshape((levels, lat_rows, lon_cols) + trailing)

def attend(normed, allowed, bias_table, project, output):
    windows, tokens_win, features = normed.shape
    head_count = bias_table.shape[0]
    head_size = features // head_count
    packed = jnp.dot(normed, project, preferred_element_type=jnp.float32).astype(jnp.bfloat16)
    packed = packed.reshape(windows, tokens_win, 3, head_count, head_size)
    queries = packed[:, :, 0].astype(jnp.float32)
    keys_all = packed[:, :, 1].astype(jnp.float32)
    values = packed[:, :, 2].astype(jnp.float32)
    scores = jnp.einsum('wqhd,wkhd->whqk', queries, keys_all) * head_size ** (-0.5) + bias_table.astype(jnp.float32)
    weights = jnp.exp(scores)
    if allowed is not None:
        weights = weights * allowed[:, None]
    probability = (weights / lax.optimization_barrier(jnp.sum(weights, axis=-1, keepdims=True))).astype(jnp.bfloat16)
    heads_out = jnp.einsum('whqk,wkhd->wqhd', probability.astype(jnp.float32), values).astype(jnp.bfloat16)
    return jnp.dot(heads_out.reshape(windows, tokens_win, features), output, preferred_element_type=jnp.float32)

def windowed(normed, group_ids, bias_table, project, output, batches):
    windows = normed.shape[0]
    normed_sets = normed.reshape((batches, windows // batches) + normed.shape[1:])
    if group_ids is None:

        def per_batch(pieces):
            return attend(pieces, None, bias_table, project, output)
        result = lax.map(jax.checkpoint(per_batch), normed_sets)
    else:
        group_sets = group_ids.reshape((batches, windows // batches) + group_ids.shape[1:])

        def per_batch(pieces):
            allowed = (pieces[1][:, :, None] == pieces[1][:, None, :]).astype(jnp.float32)
            return attend(pieces[0], allowed, bias_table, project, output)
        result = lax.map(jax.checkpoint(per_batch), (normed_sets, group_sets))
    return result.reshape((windows,) + result.shape[2:])

def reference(tokens, labels, gain_one, project_one, output_one, bias_one, gain_two, project_two, output_two, bias_two, gain_three, up_weight, down_weight, cotangent):
    levels, lat_rows, lon_cols, features = tokens.shape
    half_lat = WLAT // 2
    half_lon = WLON // 2
    batches = lat_rows // WLAT
    token_count = levels * lat_rows * lon_cols
    row_index = jnp.arange(lat_rows, dtype=jnp.int32)
    pole_side = (row_index >= lat_rows - half_lat).astype(jnp.int32)
    rolled_labels = jnp.roll(labels, (-half_lat, -half_lon), axis=(1, 2))
    group_ids = to_windows(rolled_labels * 2 + pole_side[None, :, None], WLAT, WLON)

    def feed_forward(late_in):
        normed = normalize(late_in, gain_three)
        hidden = jax.nn.gelu(jnp.dot(normed, up_weight, preferred_element_type=jnp.float32), approximate=True).astype(jnp.bfloat16)
        return late_in + jnp.dot(hidden, down_weight, preferred_element_type=jnp.float32)

    def forward(field_in):
        normed = normalize(field_in, gain_one)
        first_out = windowed(to_windows(normed, WLAT, WLON), None, bias_one, project_one, output_one, batches)
        middle = field_in + from_windows(first_out, levels, lat_rows, lon_cols, WLAT, WLON)
        normed = normalize(middle, gain_two)
        shifted = jnp.roll(normed, (-half_lat, -half_lon), axis=(1, 2))
        second = windowed(to_windows(shifted, WLAT, WLON), group_ids, bias_two, project_two, output_two, batches)
        second = jnp.roll(from_windows(second, levels, lat_rows, lon_cols, WLAT, WLON), (half_lat, half_lon), axis=(1, 2))
        late_sum = (middle + second).reshape(batches, token_count // batches, features)
        result = lax.map(jax.checkpoint(feed_forward), late_sum)
        return result.reshape(levels, lat_rows, lon_cols, features)
    result, pullback = jax.vjp(forward, tokens.astype(jnp.float32))
    gradient = pullback(cotangent.astype(jnp.float32))[0]
    return (result.astype(jnp.bfloat16), gradient.astype(jnp.bfloat16))
```

```python
import functools

import jax
import jax.numpy as jnp
import numpy as np
from jax import lax
from jax.experimental import pallas as pl
from jax.experimental.pallas import tpu as pltpu
from jax.sharding import PartitionSpec as P

MESH = pl.DeviceIdType.MESH
BF = jnp.bfloat16
F32 = jnp.float32

WLAT = 6
WLON = 12
LEV = 2
WT = LEV * WLAT * WLON
QUAD = WT // 4
SLOT = 48
ROWS = 4 * SLOT
D = 512
FF = 2048
HEADS = 16
HD = D // HEADS
LANES = 128
PER = LANES // HD
GROUPS = D // LANES
SCALE = HD ** (-0.5)
EPSILON = 1e-05


def quadrant_matrix():
    place = np.zeros((ROWS, WT), np.float32)
    hl, hc = WLAT // 2, WLON // 2
    for half_row in range(2):
        for half_col in range(2):
            for i in range(QUAD):
                level, r, c = i // (hl * hc), i // hc % hl, i % hc
                token = level * WLAT * WLON + (half_row * hl + r) * WLON + half_col * hc + c
                place[SLOT * (2 * half_row + half_col) + i, token] = 1.0
    return place


def nn(a, b):
    return lax.dot_general(a, b, (((1,), (0,)), ((), ())), preferred_element_type=F32)


def nt(a, b):
    return lax.dot_general(a, b, (((1,), (1,)), ((), ())), preferred_element_type=F32)


def tn(a, b):
    return lax.dot_general(a, b, (((0,), (0,)), ((), ())), preferred_element_type=F32)


def norm_parts(x):
    centred = x - jnp.mean(x, axis=-1, keepdims=True)
    rs = lax.rsqrt(jnp.mean(centred * centred, axis=-1, keepdims=True) + EPSILON)
    return centred * rs, rs


def norm_back(hat, rs, gain, dy):
    t = dy * gain
    return rs * (
        t - jnp.mean(t, axis=-1, keepdims=True) - hat * jnp.mean(t * hat, axis=-1, keepdims=True)
    )


def head_masks():
    lane = lax.broadcasted_iota(jnp.int32, (WT, LANES), 1)
    return [jnp.logical_and(lane >= HD * j, lane < HD * (j + 1)) for j in range(PER)]


def pick(stack, masks):
    out = stack[:WT]
    for j in range(1, PER):
        out = jnp.where(masks[j], stack[WT * j : WT * (j + 1)], out)
    return out


def spread(group, masks):
    zero = jnp.zeros_like(group)
    return jnp.concatenate([jnp.where(m, group, zero) for m in masks], axis=0)


def attention(packed, bias, probs, heads, allowed, masks):
    for g in range(GROUPS):
        lanes = slice(LANES * g, LANES * (g + 1))
        q = packed[:, LANES * g : LANES * (g + 1)]
        k = packed[:, D + LANES * g : D + LANES * (g + 1)]
        v = packed[:, 2 * D + LANES * g : 2 * D + LANES * (g + 1)]
        s = nt(spread(q, masks), k)
        for j in range(PER):
            h = PER * g + j
            e = jnp.exp(s[WT * j : WT * (j + 1)] * SCALE + bias[h].astype(F32))
            if allowed is not None:
                e = e * allowed
            z = jnp.sum(e, axis=-1, keepdims=True)
            down = jnp.where(z > 2.0**64, 2.0**-64, 1.0).astype(F32)
            probs[pl.ds(WT * h, WT), :] = ((e * down) * (1.0 / (z * down))).astype(BF)
        o = nn(probs[pl.ds(WT * PER * g, WT * PER), :], v)
        heads[:, lanes] = pick(o, masks).astype(BF)


def attention_back(packed, probs, heads, d_heads, d_packed, masks):
    for g in range(GROUPS):
        q = packed[:, LANES * g : LANES * (g + 1)]
        k = packed[:, D + LANES * g : D + LANES * (g + 1)]
        v = packed[:, 2 * D + LANES * g : 2 * D + LANES * (g + 1)]
        do = d_heads[:, LANES * g : LANES * (g + 1)]
        o = heads[:, LANES * g : LANES * (g + 1)]
        less = (-(do.astype(F32) * o.astype(F32))).astype(BF)
        do_stack = spread(do, masks)
        left = jnp.concatenate([do_stack, spread(less, masks)], axis=1)
        right = jnp.concatenate([v, jnp.ones_like(v)], axis=1)
        dp = nt(left, right)
        p = probs[pl.ds(WT * PER * g, WT * PER), :]
        ds = (p.astype(F32) * dp).astype(BF)
        dq = pick(nn(ds, k), masks) * SCALE
        dk = tn(ds, spread(q, masks)) * SCALE
        dv = tn(p, do_stack)
        d_packed[:, LANES * g : LANES * (g + 1)] = dq.astype(BF)
        d_packed[:, D + LANES * g : D + LANES * (g + 1)] = dk.astype(BF)
        d_packed[:, 2 * D + LANES * g : 2 * D + LANES * (g + 1)] = dv.astype(BF)


def kernel(
    n_lat, n_lon,
    tokens, labels, gain_one, project_one, output_one, bias_one, gain_two, project_two, output_two,
    bias_two, gain_three, up_weight, down_weight, cotangent, to_quad, from_quad,
    outputs, input_grad,
    tok, lab, g1, w1, wo1, b1, g2, w2, wo2, b2, g3, wup, wdn, cot, tq, fq,
    x, ct, packed_one, packed_two, probs_one, probs_two, heads_one, heads_two, d_heads, d_packed,
    middle, hat_one, hat_two, u_keep, dh_keep, result, allowed_ref,
    out_stage, grad_stage,
    send, recv, lab_send, lab_recv,
    load_sem, send_sem, recv_sem, lab_send_sem, lab_recv_sem, out_sem,
):
    i = lax.axis_index("lat")
    j = lax.axis_index("lon")
    north, south = lax.rem(i + n_lat - 1, n_lat), lax.rem(i + 1, n_lat)
    west, east = lax.rem(j + n_lon - 1, n_lon), lax.rem(j + 1, n_lon)
    barrier = pltpu.get_barrier_semaphore()
    around = [(i, east), (south, j), (south, east), (i, west), (north, j), (north, west)]
    for device in around:
        pl.semaphore_signal(barrier, inc=1, device_id=device, device_id_type=MESH)

    pairs = {
        "tok": (tokens, tok), "g1": (gain_one, g1), "w1": (project_one, w1), "b1": (bias_one, b1),
        "lab": (labels, lab), "tq": (to_quad, tq), "fq": (from_quad, fq),
        "wo1": (output_one, wo1), "g2": (gain_two, g2), "cot": (cotangent, cot), "w2": (project_two, w2),
        "wdn": (down_weight, wdn), "b2": (bias_two, b2),
        "wo2": (output_two, wo2), "g3": (gain_three, g3), "wup": (up_weight, wup),
    }
    loads = {}
    for at, (name, (source, target)) in enumerate(pairs.items()):
        loads[name] = pltpu.make_async_copy(source, target, load_sem.at[at])
        loads[name].start()

    masks = head_masks()

    def to_rows(source, target):
        for a in range(LEV):
            for b in range(WLAT):
                target[pl.ds((a * WLAT + b) * WLON, WLON), :] = source[a, b].astype(F32)

    owner_target = {0: (north, west), 1: (north, j), 2: (i, west)}
    window_target = {3: (south, east), 2: (south, j), 1: (i, east)}

    def exchange(step, targets):
        copies = []
        for q, device in targets.items():
            copies.append(
                pltpu.make_async_remote_copy(
                    src_ref=send.at[step, pl.ds(SLOT * q, SLOT)],
                    dst_ref=recv.at[step, pl.ds(SLOT * (3 - q), SLOT)],
                    send_sem=send_sem.at[step, q],
                    recv_sem=recv_sem.at[step, q],
                    device_id=device,
                    device_id_type=MESH,
                )
            )
        return copies

    def start(step, targets, value):
        rows = nn(tq[...], value).astype(BF)
        send[step] = rows
        stay = 3 if step % 2 == 0 else 0
        recv[step, pl.ds(SLOT * (3 - stay), SLOT)] = rows[SLOT * stay : SLOT * (stay + 1)]
        copies = exchange(step, targets)
        for copy in copies:
            copy.start()
        return copies

    def arrived(step, copies):
        for copy in copies:
            copy.wait_recv()
        return nn(fq[...], recv[step]).astype(BF)

    loads["tok"].wait()
    to_rows(tok, x)
    loads["g1"].wait()
    hat, rs_one = norm_parts(x[...])
    hat_one[...] = hat
    normed = (hat * g1[...]).astype(BF)
    loads["w1"].wait()
    packed_one[...] = nn(normed, w1[...]).astype(BF)

    loads["lab"].wait()
    loads["tq"].wait()
    loads["fq"].wait()
    token = lax.broadcasted_iota(jnp.int32, (WT, WLON), 0)
    column = lax.broadcasted_iota(jnp.int32, (WT, WLON), 1)
    labelled = jnp.zeros((WT, WLON), F32)
    for a in range(LEV):
        level = lab[a].astype(F32)
        for b in range(WLAT):
            line = jnp.broadcast_to(level[b : b + 1, :], (WT, WLON))
            labelled = jnp.where(token - (a * WLAT + b) * WLON == column, line, labelled)
    label_col = jnp.sum(labelled, axis=-1, keepdims=True)
    label_rows = nn(tq[...], jnp.broadcast_to(label_col, (WT, LANES)).astype(BF)).astype(BF)
    lab_send[...] = label_rows
    lab_recv[pl.ds(0, SLOT)] = label_rows[3 * SLOT :]
    pl.semaphore_wait(barrier, len(around))
    lab_copies = []
    for q, device in owner_target.items():
        lab_copies.append(
            pltpu.make_async_remote_copy(
                src_ref=lab_send.at[pl.ds(SLOT * q, SLOT)],
                dst_ref=lab_recv.at[pl.ds(SLOT * (3 - q), SLOT)],
                send_sem=lab_send_sem.at[q],
                recv_sem=lab_recv_sem.at[q],
                device_id=device,
                device_id_type=MESH,
            )
        )
        lab_copies[-1].start()

    loads["b1"].wait()
    attention(packed_one, b1, probs_one, heads_one, None, masks)
    loads["wo1"].wait()
    mid = x[...] + nn(heads_one[...], wo1[...])
    middle[...] = mid
    hat, rs_two = norm_parts(mid)
    hat_two[...] = hat
    loads["g2"].wait()
    copies_0 = start(0, owner_target, (hat * g2[...]).astype(BF))

    loads["cot"].wait()
    to_rows(cot, ct)
    loads["wdn"].wait()
    dh_keep[...] = nt(ct[...].astype(BF), wdn[...]).astype(BF)
    for copy in lab_copies:
        copy.wait_recv()
    label_here = nn(fq[...], lab_recv[...])
    row = lax.broadcasted_iota(jnp.int32, (WT, LANES), 0)
    half = WLAT * WLON
    late_row = jnp.logical_or(
        jnp.logical_and(row >= half // 2, row < half), row >= half + half // 2
    )
    edge = jnp.where(i == n_lat - 1, 1.0, 0.0).astype(F32)
    ids = label_here * 2.0 + jnp.where(late_row, edge, 0.0)
    lane = lax.broadcasted_iota(jnp.int32, (WT, LANES), 1).astype(F32)
    one_hot = jnp.where(ids == lane, 1.0, 0.0).astype(BF)
    allowed_ref[...] = nt(one_hot, one_hot)

    loads["w2"].wait()
    loads["b2"].wait()
    normed = arrived(0, copies_0)

    packed_two[...] = nn(normed, w2[...]).astype(BF)
    attention(packed_two, b2, probs_two, heads_two, allowed_ref[...], masks)
    copies_1 = start(1, window_target, heads_two[...])
    loads["wo2"].wait()
    loads["g3"].wait()
    loads["wup"].wait()
    late = middle[...] + nn(arrived(1, copies_1), wo2[...])

    hat, rs_three = norm_parts(late)
    u = nn((hat * g3[...]).astype(BF), wup[...])
    root = (2.0 / np.pi) ** 0.5
    square = u * u
    bent = jnp.tanh(root * u * (1.0 + 0.044715 * square))
    slope = 0.5 * (1.0 + bent) + (0.5 * root) * u * (1.0 - bent * bent) * (
        1.0 + (3.0 * 0.044715) * square
    )
    du = (dh_keep[...].astype(F32) * slope).astype(BF)
    hidden = (0.5 * u * (1.0 + bent)).astype(BF)
    u_keep[...] = hidden
    dn = nt(du, wup[...]).astype(BF).astype(F32)
    d_late = ct[...] + norm_back(hat, rs_three, g3[...], dn)
    copies_2 = start(2, owner_target, nt(d_late.astype(BF), wo2[...]).astype(BF))

    result[...] = late + nn(u_keep[...], wdn[...])
    for a in range(LEV):
        for b in range(WLAT):
            out_stage[a, b] = result[pl.ds((a * WLAT + b) * WLON, WLON), :].astype(BF)
    out_copy = pltpu.make_async_copy(out_stage, outputs, out_sem.at[0])
    out_copy.start()

    d_heads[...] = arrived(2, copies_2)
    attention_back(packed_two, probs_two, heads_two, d_heads, d_packed, masks)
    copies_3 = start(3, window_target, nt(d_packed[...], w2[...]).astype(BF))
    dn = arrived(3, copies_3).astype(F32)
    d_mid = d_late + norm_back(hat_two[...], rs_two, g2[...], dn)

    d_heads[...] = nt(d_mid.astype(BF), wo1[...]).astype(BF)
    attention_back(packed_one, probs_one, heads_one, d_heads, d_packed, masks)
    dn = nt(d_packed[...], w1[...]).astype(BF).astype(F32)
    result[...] = d_mid + norm_back(hat_one[...], rs_one, g1[...], dn)
    for a in range(LEV):
        for b in range(WLAT):
            grad_stage[a, b] = result[pl.ds((a * WLAT + b) * WLON, WLON), :].astype(BF)
    grad_copy = pltpu.make_async_copy(grad_stage, input_grad, out_sem.at[1])
    grad_copy.start()
    for copy in lab_copies + copies_0 + copies_1 + copies_2 + copies_3:
        copy.wait_send()
    out_copy.wait()
    grad_copy.wait()


def per_device(n_lat, n_lon, *args):
    (tokens, labels, g1, w1, wo1, b1, g2, w2, wo2, b2, g3, wup, wdn, cot) = args
    place = quadrant_matrix()
    to_quad = jnp.asarray(place, BF)
    from_quad = jnp.asarray(place.T, BF)
    operands = (
        tokens, labels, g1.reshape(1, D), w1, wo1, b1, g2.reshape(1, D), w2, wo2, b2,
        g3.reshape(1, D), wup, wdn, cot, to_quad, from_quad,
    )
    vm = pltpu.VMEM
    landing = [vm(a.shape, a.dtype) for a in operands]
    block = tokens.shape
    scratch = landing + [
        vm((WT, D), F32), vm((WT, D), F32),
        vm((WT, 3 * D), BF), vm((WT, 3 * D), BF),
        vm((HEADS * WT, WT), BF), vm((HEADS * WT, WT), BF),
        vm((WT, D), BF), vm((WT, D), BF), vm((WT, D), BF), vm((WT, 3 * D), BF),
        vm((WT, D), F32), vm((WT, D), F32), vm((WT, D), F32),
        vm((WT, FF), BF), vm((WT, FF), BF), vm((WT, D), F32), vm((WT, WT), F32),
        vm(block, BF), vm(block, BF),
        vm((4, ROWS, D), BF), vm((4, ROWS, D), BF), vm((ROWS, LANES), BF), vm((ROWS, LANES), BF),
        pltpu.SemaphoreType.DMA((len(operands),)),
        pltpu.SemaphoreType.DMA((4, 4)), pltpu.SemaphoreType.DMA((4, 4)),
        pltpu.SemaphoreType.DMA((4,)), pltpu.SemaphoreType.DMA((4,)),
        pltpu.SemaphoreType.DMA((2,)),
    ]
    whole = pl.BlockSpec(memory_space=pl.ANY)
    return pl.pallas_call(
        functools.partial(kernel, n_lat, n_lon),
        out_shape=(jax.ShapeDtypeStruct(block, BF), jax.ShapeDtypeStruct(block, BF)),
        in_specs=[whole] * len(operands),
        out_specs=(whole, whole),
        scratch_shapes=scratch,
        compiler_params=pltpu.CompilerParams(
            collective_id=0, has_side_effects=True, vmem_limit_bytes=56 * 1024 * 1024
        ),
    )(*operands)


def solution(mesh):
    field = P(None, "lat", "lon", None)
    return jax.shard_map(
        functools.partial(per_device, mesh.shape["lat"], mesh.shape["lon"]),
        mesh=mesh,
        in_specs=(field, P(None, "lat", "lon")) + (P(),) * 11 + (field,),
        out_specs=(field, field),
        check_vma=False,
    )
```

```python
import functools

import jax
import jax.numpy as jnp
import numpy as np
from jax import lax
from jax.experimental import pallas as pl
from jax.experimental.pallas import tpu as pltpu
from jax.sharding import PartitionSpec as P

MESH = pl.DeviceIdType.MESH
BF = jnp.bfloat16
F32 = jnp.float32

WLAT = 6
WLON = 12
LEV = 2
PLANE = WLAT * WLON
WT = LEV * PLANE
QUAD = WT // 4
SLOT = 48
ROWS = 4 * SLOT
D = 512
FF = 2048
HEADS = 16
HD = D // HEADS
LANES = 128
PER = LANES // HD
GROUPS = D // LANES
SCALE = HD ** (-0.5)
EPSILON = 1e-05


def quadrant_matrix():
    place = np.zeros((ROWS, WT), np.float32)
    hl, hc = WLAT // 2, WLON // 2
    for half_row in range(2):
        for half_col in range(2):
            for i in range(QUAD):
                level, r, c = i // (hl * hc), i // hc % hl, i % hc
                token = level * WLAT * WLON + (half_row * hl + r) * WLON + half_col * hc + c
                place[SLOT * (2 * half_row + half_col) + i, token] = 1.0
    return place


def nn(a, b):
    return lax.dot_general(a, b, (((1,), (0,)), ((), ())), preferred_element_type=F32)


def nt(a, b):
    return lax.dot_general(a, b, (((1,), (1,)), ((), ())), preferred_element_type=F32)


def tn(a, b):
    return lax.dot_general(a, b, (((0,), (0,)), ((), ())), preferred_element_type=F32)


def norm_parts(x):
    centred = x - jnp.mean(x, axis=-1, keepdims=True)
    rs = lax.rsqrt(jnp.mean(centred * centred, axis=-1, keepdims=True) + EPSILON)
    return centred * rs, rs


def norm_back(hat, rs, gain, dy):
    t = dy * gain
    return rs * (
        t - jnp.mean(t, axis=-1, keepdims=True) - hat * jnp.mean(t * hat, axis=-1, keepdims=True)
    )


def head_masks():
    lane = lax.broadcasted_iota(jnp.int32, (WT, LANES), 1)
    return [jnp.logical_and(lane >= HD * j, lane < HD * (j + 1)) for j in range(PER)]


def pick(stack, masks):
    out = stack[:WT]
    for j in range(1, PER):
        out = jnp.where(masks[j], stack[WT * j : WT * (j + 1)], out)
    return out


def spread(group, masks):
    zero = jnp.zeros_like(group)
    return jnp.concatenate([jnp.where(m, group, zero) for m in masks], axis=0)


def attention(packed, bias, probs, heads, allowed, masks):
    for g in range(GROUPS):
        lanes = slice(LANES * g, LANES * (g + 1))
        q = packed[:, LANES * g : LANES * (g + 1)]
        k = packed[:, D + LANES * g : D + LANES * (g + 1)]
        v = packed[:, 2 * D + LANES * g : 2 * D + LANES * (g + 1)]
        s = nt(spread(q, masks), k)
        for j in range(PER):
            h = PER * g + j
            e = jnp.exp(s[WT * j : WT * (j + 1)] * SCALE + bias[h].astype(F32))
            if allowed is not None:
                e = e * allowed
            z = jnp.sum(e, axis=-1, keepdims=True)
            down = jnp.where(z > 2.0**64, 2.0**-64, 1.0).astype(F32)
            probs[pl.ds(WT * h, WT), :] = ((e * down) * (1.0 / (z * down))).astype(BF)
        o = nn(probs[pl.ds(WT * PER * g, WT * PER), :], v)
        heads[:, lanes] = pick(o, masks).astype(BF)


def attention_back(packed, probs, heads, d_heads, d_packed, masks):
    for g in range(GROUPS):
        q = packed[:, LANES * g : LANES * (g + 1)]
        k = packed[:, D + LANES * g : D + LANES * (g + 1)]
        v = packed[:, 2 * D + LANES * g : 2 * D + LANES * (g + 1)]
        do = d_heads[:, LANES * g : LANES * (g + 1)]
        o = heads[:, LANES * g : LANES * (g + 1)]
        less = (-(do.astype(F32) * o.astype(F32))).astype(BF)
        do_stack = spread(do, masks)
        left = jnp.concatenate([do_stack, spread(less, masks)], axis=1)
        right = jnp.concatenate([v, jnp.ones_like(v)], axis=1)
        dp = nt(left, right)
        p = probs[pl.ds(WT * PER * g, WT * PER), :]
        ds = (p.astype(F32) * dp).astype(BF)
        dq = pick(nn(ds, k), masks) * SCALE
        dk = tn(ds, spread(q, masks)) * SCALE
        dv = tn(p, do_stack)
        d_packed[:, LANES * g : LANES * (g + 1)] = dq.astype(BF)
        d_packed[:, D + LANES * g : D + LANES * (g + 1)] = dk.astype(BF)
        d_packed[:, 2 * D + LANES * g : 2 * D + LANES * (g + 1)] = dv.astype(BF)


def kernel(
    n_lat, n_lon,
    tokens, labels, gain_one, project_one, output_one, bias_one, gain_two, project_two, output_two,
    bias_two, gain_three, up_weight, down_weight, cotangent, to_quad, from_quad,
    outputs, input_grad,
    tok, lab, g1, w1, wo1, b1, g2, w2, wo2, b2, g3, wup, wdn, cot, tq, fq,
    x, ct, packed_one, packed_two, probs_one, probs_two, heads_one, heads_two, d_heads, d_packed,
    hat_one, hat_two, hidden, dh_keep, allowed_ref,
    out_stage, grad_stage,
    send, recv, lab_send, lab_recv,
    load_sem, send_sem, recv_sem, lab_send_sem, lab_recv_sem, out_sem,
):
    i = lax.axis_index("lat")
    j = lax.axis_index("lon")
    north, south = lax.rem(i + n_lat - 1, n_lat), lax.rem(i + 1, n_lat)
    west, east = lax.rem(j + n_lon - 1, n_lon), lax.rem(j + 1, n_lon)
    barrier = pltpu.get_barrier_semaphore()
    around = [(i, east), (south, j), (south, east), (i, west), (north, j), (north, west)]
    for device in around:
        pl.semaphore_signal(barrier, inc=1, device_id=device, device_id_type=MESH)

    pairs = {
        "tok": (tokens, tok), "g1": (gain_one, g1), "w1": (project_one, w1), "b1": (bias_one, b1),
        "lab": (labels, lab), "tq": (to_quad, tq), "fq": (from_quad, fq),
        "wo1": (output_one, wo1), "g2": (gain_two, g2), "cot": (cotangent, cot), "w2": (project_two, w2),
        "wdn": (down_weight, wdn), "b2": (bias_two, b2),
        "wo2": (output_two, wo2), "g3": (gain_three, g3), "wup": (up_weight, wup),
    }
    loads = {}
    for at, (name, (source, target)) in enumerate(pairs.items()):
        loads[name] = pltpu.make_async_copy(source, target, load_sem.at[at])
        loads[name].start()

    masks = head_masks()

    def to_rows(source, target):
        for level in range(LEV):
            target[pl.ds(PLANE * level, PLANE), :] = source[:, level, :].astype(F32)

    def to_cells(value, target):
        for level in range(LEV):
            target[:, level, :] = value[PLANE * level : PLANE * (level + 1)].astype(BF)

    owner_target = {0: (north, west), 2: (i, west), 1: (north, j)}
    window_target = {3: (south, east), 1: (i, east), 2: (south, j)}

    def start(step, targets, value):
        rows = nn(tq[...], value).astype(BF)
        send[step] = rows
        stay = 3 if targets is owner_target else 0
        recv[step, pl.ds(SLOT * (3 - stay), SLOT)] = rows[SLOT * stay : SLOT * (stay + 1)]
        copies = []
        for q, device in targets.items():
            copies.append(
                pltpu.make_async_remote_copy(
                    src_ref=send.at[step, pl.ds(SLOT * q, SLOT)],
                    dst_ref=recv.at[step, pl.ds(SLOT * (3 - q), SLOT)],
                    send_sem=send_sem.at[step, q],
                    recv_sem=recv_sem.at[step, q],
                    device_id=device,
                    device_id_type=MESH,
                )
            )
            copies[-1].start()
        return copies

    def arrived(step, copies):
        for copy in copies:
            copy.wait_recv()
        return nn(fq[...], recv[step])

    loads["tok"].wait()
    to_rows(tok, x)
    loads["g1"].wait()
    hat, rs_one = norm_parts(x[...])
    hat_one[...] = hat
    normed = (hat * g1[...]).astype(BF)
    loads["w1"].wait()
    packed_one[...] = nn(normed, w1[...]).astype(BF)

    for name in ("lab", "tq", "fq", "cot"):
        loads[name].wait()
    token = lax.broadcasted_iota(jnp.int32, (WT, WLON), 0)
    column = lax.broadcasted_iota(jnp.int32, (WT, WLON), 1)
    labelled = jnp.zeros((WT, WLON), F32)
    for b in range(WLAT):
        line_pair = lab[b].astype(F32)
        for a in range(LEV):
            line = jnp.broadcast_to(line_pair[a : a + 1, :], (WT, WLON))
            labelled = jnp.where(token - (a * WLAT + b) * WLON == column, line, labelled)
    label_col = jnp.sum(labelled, axis=-1, keepdims=True)
    label_rows = nn(tq[...], jnp.broadcast_to(label_col, (WT, LANES)).astype(BF)).astype(BF)
    lab_send[...] = label_rows
    lab_recv[pl.ds(0, SLOT)] = label_rows[3 * SLOT :]
    to_rows(cot, ct)
    pl.semaphore_wait(barrier, len(around))
    lab_copies = []
    for q, device in owner_target.items():
        lab_copies.append(
            pltpu.make_async_remote_copy(
                src_ref=lab_send.at[pl.ds(SLOT * q, SLOT)],
                dst_ref=lab_recv.at[pl.ds(SLOT * (3 - q), SLOT)],
                send_sem=lab_send_sem.at[q],
                recv_sem=lab_recv_sem.at[q],
                device_id=device,
                device_id_type=MESH,
            )
        )
        lab_copies[-1].start()
    cot_copies = start(0, owner_target, ct[...].astype(BF))

    loads["b1"].wait()
    attention(packed_one, b1, probs_one, heads_one, None, masks)
    loads["wo1"].wait()
    mid_copies = start(1, owner_target, (x[...] + nn(heads_one[...], wo1[...])).astype(BF))

    ct[...] = arrived(0, cot_copies)
    loads["wdn"].wait()
    dh_keep[...] = nt(ct[...].astype(BF), wdn[...]).astype(BF)
    for copy in lab_copies:
        copy.wait_recv()
    label_here = nn(fq[...], lab_recv[...])
    row = lax.broadcasted_iota(jnp.int32, (WT, LANES), 0)
    late_row = jnp.logical_or(
        jnp.logical_and(row >= PLANE // 2, row < PLANE), row >= PLANE + PLANE // 2
    )
    edge = jnp.where(i == n_lat - 1, 1.0, 0.0).astype(F32)
    ids = label_here * 2.0 + jnp.where(late_row, edge, 0.0)
    lane = lax.broadcasted_iota(jnp.int32, (WT, LANES), 1).astype(F32)
    one_hot = jnp.where(ids == lane, 1.0, 0.0).astype(BF)
    allowed_ref[...] = nt(one_hot, one_hot)
    for name in ("g2", "w2", "b2", "wo2", "g3", "wup"):
        loads[name].wait()

    mid = arrived(1, mid_copies)
    hat, rs_two = norm_parts(mid)
    hat_two[...] = hat
    packed_two[...] = nn((hat * g2[...]).astype(BF), w2[...]).astype(BF)
    attention(packed_two, b2, probs_two, heads_two, allowed_ref[...], masks)
    late = mid + nn(heads_two[...], wo2[...])

    hat, rs_three = norm_parts(late)
    u = nn((hat * g3[...]).astype(BF), wup[...])
    root = (2.0 / np.pi) ** 0.5
    square = u * u
    bent = jnp.tanh(root * u * (1.0 + 0.044715 * square))
    slope = 0.5 * (1.0 + bent) + (0.5 * root) * u * (1.0 - bent * bent) * (
        1.0 + (3.0 * 0.044715) * square
    )
    du = (dh_keep[...].astype(F32) * slope).astype(BF)
    hidden[...] = (0.5 * u * (1.0 + bent)).astype(BF)
    dn = nt(du, wup[...]).astype(BF).astype(F32)
    d_late = ct[...] + norm_back(hat, rs_three, g3[...], dn)

    d_heads[...] = nt(d_late.astype(BF), wo2[...]).astype(BF)
    attention_back(packed_two, probs_two, heads_two, d_heads, d_packed, masks)
    dn = nt(d_packed[...], w2[...]).astype(BF).astype(F32)
    d_mid = d_late + norm_back(hat_two[...], rs_two, g2[...], dn)
    back_copies = start(2, window_target, d_mid.astype(BF))
    out_copies = start(3, window_target, (late + nn(hidden[...], wdn[...])).astype(BF))

    d_mid = arrived(2, back_copies)
    d_heads[...] = nt(d_mid.astype(BF), wo1[...]).astype(BF)
    attention_back(packed_one, probs_one, heads_one, d_heads, d_packed, masks)
    to_cells(arrived(3, out_copies), out_stage)
    out_copy = pltpu.make_async_copy(out_stage, outputs, out_sem.at[0])
    out_copy.start()
    dn = nt(d_packed[...], w1[...]).astype(BF).astype(F32)
    to_cells(d_mid + norm_back(hat_one[...], rs_one, g1[...], dn), grad_stage)
    grad_copy = pltpu.make_async_copy(grad_stage, input_grad, out_sem.at[1])
    grad_copy.start()
    for copy in lab_copies + cot_copies + mid_copies + back_copies + out_copies:
        copy.wait_send()
    out_copy.wait()
    grad_copy.wait()


def per_device(n_lat, n_lon, *args):
    (tokens, labels, g1, w1, wo1, b1, g2, w2, wo2, b2, g3, wup, wdn, cot) = args
    place = quadrant_matrix()
    to_quad = jnp.asarray(place, BF)
    from_quad = jnp.asarray(place.T, BF)
    def cells(a):
        return a.transpose(1, 2, 0, 3).reshape(PLANE, LEV, D)

    operands = (
        cells(tokens), labels.transpose(1, 0, 2), g1.reshape(1, D), w1, wo1, b1, g2.reshape(1, D), w2, wo2, b2,
        g3.reshape(1, D), wup, wdn, cells(cot), to_quad, from_quad,
    )
    vm = pltpu.VMEM
    landing = [vm(a.shape, a.dtype) for a in operands]
    block = (PLANE, LEV, D)
    scratch = landing + [
        vm((WT, D), F32), vm((WT, D), F32),
        vm((WT, 3 * D), BF), vm((WT, 3 * D), BF),
        vm((HEADS * WT, WT), BF), vm((HEADS * WT, WT), BF),
        vm((WT, D), BF), vm((WT, D), BF), vm((WT, D), BF), vm((WT, 3 * D), BF),
        vm((WT, D), F32), vm((WT, D), F32), vm((WT, FF), BF), vm((WT, FF), BF), vm((WT, WT), F32),
        vm(block, BF), vm(block, BF),
        vm((4, ROWS, D), BF), vm((4, ROWS, D), BF), vm((ROWS, LANES), BF), vm((ROWS, LANES), BF),
        pltpu.SemaphoreType.DMA((len(operands),)),
        pltpu.SemaphoreType.DMA((4, 4)), pltpu.SemaphoreType.DMA((4, 4)),
        pltpu.SemaphoreType.DMA((4,)), pltpu.SemaphoreType.DMA((4,)),
        pltpu.SemaphoreType.DMA((2,)),
    ]
    whole = pl.BlockSpec(memory_space=pl.ANY)
    results = pl.pallas_call(
        functools.partial(kernel, n_lat, n_lon),
        out_shape=(jax.ShapeDtypeStruct(block, BF), jax.ShapeDtypeStruct(block, BF)),
        in_specs=[whole] * len(operands),
        out_specs=(whole, whole),
        scratch_shapes=scratch,
        compiler_params=pltpu.CompilerParams(
            collective_id=0, has_side_effects=True, vmem_limit_bytes=56 * 1024 * 1024
        ),
    )(*operands)
    return tuple(a.reshape(WLAT, WLON, LEV, D).transpose(2, 0, 1, 3) for a in results)


def solution(mesh):
    field = P(None, "lat", "lon", None)
    return jax.shard_map(
        functools.partial(per_device, mesh.shape["lat"], mesh.shape["lon"]),
        mesh=mesh,
        in_specs=(field, P(None, "lat", "lon")) + (P(),) * 11 + (field,),
        out_specs=(field, field),
        check_vma=False,
    )
```

```python
import functools

import jax
import jax.numpy as jnp
import numpy as np
from jax import lax
from jax.experimental import pallas as pl
from jax.experimental.pallas import tpu as pltpu
from jax.sharding import PartitionSpec as P

MESH = pl.DeviceIdType.MESH
BF = jnp.bfloat16
F32 = jnp.float32

WLAT = 6
WLON = 12
LEV = 2
PLANE = WLAT * WLON
WT = LEV * PLANE
QUAD = WT // 4
SLOT = 48
ROWS = 4 * SLOT
D = 512
FF = 2048
HEADS = 16
HD = D // HEADS
LANES = 128
PER = LANES // HD
GROUPS = D // LANES
SCALE = HD ** (-0.5)
EPSILON = 1e-05


def quadrant_matrix():
    place = np.zeros((ROWS, WT), np.float32)
    hl, hc = WLAT // 2, WLON // 2
    for half_row in range(2):
        for half_col in range(2):
            for i in range(QUAD):
                level, r, c = i // (hl * hc), i // hc % hl, i % hc
                token = level * WLAT * WLON + (half_row * hl + r) * WLON + half_col * hc + c
                place[SLOT * (2 * half_row + half_col) + i, token] = 1.0
    return place


def nn(a, b):
    return lax.dot_general(a, b, (((1,), (0,)), ((), ())), preferred_element_type=F32)


def nt(a, b):
    return lax.dot_general(a, b, (((1,), (1,)), ((), ())), preferred_element_type=F32)


def tn(a, b):
    return lax.dot_general(a, b, (((0,), (0,)), ((), ())), preferred_element_type=F32)


def norm_parts(x):
    centred = x - jnp.mean(x, axis=-1, keepdims=True)
    rs = lax.rsqrt(jnp.mean(centred * centred, axis=-1, keepdims=True) + EPSILON)
    return centred * rs, rs


def norm_back(hat, rs, gain, dy):
    t = dy * gain
    return rs * (
        t - jnp.mean(t, axis=-1, keepdims=True) - hat * jnp.mean(t * hat, axis=-1, keepdims=True)
    )


def head_masks():
    lane = lax.broadcasted_iota(jnp.int32, (WT, LANES), 1)
    return [jnp.logical_and(lane >= HD * j, lane < HD * (j + 1)) for j in range(PER)]


def pick(stack, masks):
    out = stack[:WT]
    for j in range(1, PER):
        out = jnp.where(masks[j], stack[WT * j : WT * (j + 1)], out)
    return out


def spread(group, masks):
    zero = jnp.zeros_like(group)
    return jnp.concatenate([jnp.where(m, group, zero) for m in masks], axis=0)


def attention(packed, bias, probs, heads, allowed, masks):
    for g in range(GROUPS):
        lanes = slice(LANES * g, LANES * (g + 1))
        q = packed[:, LANES * g : LANES * (g + 1)]
        k = packed[:, D + LANES * g : D + LANES * (g + 1)]
        v = packed[:, 2 * D + LANES * g : 2 * D + LANES * (g + 1)]
        s = nt(spread(q, masks), k)
        for j in range(PER):
            h = PER * g + j
            e = jnp.exp(s[WT * j : WT * (j + 1)] * SCALE + bias[h].astype(F32))
            if allowed is not None:
                e = e * allowed
            z = jnp.sum(e, axis=-1, keepdims=True)
            down = jnp.where(z > 2.0**64, 2.0**-64, 1.0).astype(F32)
            probs[pl.ds(WT * h, WT), :] = ((e * down) * (1.0 / (z * down))).astype(BF)
        o = nn(probs[pl.ds(WT * PER * g, WT * PER), :], v)
        heads[:, lanes] = pick(o, masks).astype(BF)


def attention_back(packed, probs, heads, d_heads, d_packed, masks):
    for g in range(GROUPS):
        q = packed[:, LANES * g : LANES * (g + 1)]
        k = packed[:, D + LANES * g : D + LANES * (g + 1)]
        v = packed[:, 2 * D + LANES * g : 2 * D + LANES * (g + 1)]
        do = d_heads[:, LANES * g : LANES * (g + 1)]
        o = heads[:, LANES * g : LANES * (g + 1)]
        less = (-(do.astype(F32) * o.astype(F32))).astype(BF)
        do_stack = spread(do, masks)
        left = jnp.concatenate([do_stack, spread(less, masks)], axis=1)
        right = jnp.concatenate([v, jnp.ones_like(v)], axis=1)
        dp = nt(left, right)
        p = probs[pl.ds(WT * PER * g, WT * PER), :]
        ds = (p.astype(F32) * dp).astype(BF)
        dq = pick(nn(ds, k), masks) * SCALE
        dk = tn(ds, spread(q, masks)) * SCALE
        dv = tn(p, do_stack)
        d_packed[:, LANES * g : LANES * (g + 1)] = dq.astype(BF)
        d_packed[:, D + LANES * g : D + LANES * (g + 1)] = dk.astype(BF)
        d_packed[:, 2 * D + LANES * g : 2 * D + LANES * (g + 1)] = dv.astype(BF)


def kernel(
    n_lat, n_lon,
    tokens, labels, gain_one, project_one, output_one, bias_one, gain_two, project_two, output_two,
    bias_two, gain_three, up_weight, down_weight, cotangent, to_quad, from_quad,
    outputs, input_grad,
    tok, lab, g1, w1, wo1, b1, g2, w2, wo2, b2, g3, wup, wdn, cot, tq, fq,
    x, ct, packed_one, packed_two, probs_one, probs_two, heads_one, heads_two, d_heads, d_packed,
    hat_one, hat_two, hidden, dh_keep, allowed_ref,
    out_stage, grad_stage,
    send, recv, lab_send, lab_recv,
    load_sem, send_sem, recv_sem, lab_send_sem, lab_recv_sem, out_sem,
):
    i = lax.axis_index("lat")
    j = lax.axis_index("lon")
    north, south = lax.rem(i + n_lat - 1, n_lat), lax.rem(i + 1, n_lat)
    west, east = lax.rem(j + n_lon - 1, n_lon), lax.rem(j + 1, n_lon)
    barrier = pltpu.get_barrier_semaphore()
    around = [(i, east), (south, j), (south, east), (i, west), (north, j), (north, west)]
    for device in around:
        pl.semaphore_signal(barrier, inc=1, device_id=device, device_id_type=MESH)

    pairs = {
        "tok": (tokens, tok), "g1": (gain_one, g1), "w1": (project_one, w1), "b1": (bias_one, b1),
        "lab": (labels, lab), "tq": (to_quad, tq), "fq": (from_quad, fq),
        "wo1": (output_one, wo1), "g2": (gain_two, g2), "cot": (cotangent, cot), "w2": (project_two, w2),
        "wdn": (down_weight, wdn), "b2": (bias_two, b2),
        "wo2": (output_two, wo2), "g3": (gain_three, g3), "wup": (up_weight, wup),
    }
    loads = {}
    for at, (name, (source, target)) in enumerate(pairs.items()):
        loads[name] = pltpu.make_async_copy(source, target, load_sem.at[at])
        loads[name].start()

    masks = head_masks()

    def to_rows(source, target):
        for level in range(LEV):
            target[pl.ds(PLANE * level, PLANE), :] = source[:, level, :].astype(F32)

    def to_cells(value, target):
        for level in range(LEV):
            target[:, level, :] = value[PLANE * level : PLANE * (level + 1)].astype(BF)

    owner_target = {3: (south, east), 1: (i, east), 2: (south, j)}
    window_target = {0: (north, west), 2: (i, west), 1: (north, j)}

    def start(step, targets, value):
        rows = nn(tq[...], value).astype(BF)
        send[step] = rows
        stay = 0 if targets is owner_target else 3
        recv[step, pl.ds(SLOT * (3 - stay), SLOT)] = rows[SLOT * stay : SLOT * (stay + 1)]
        copies = []
        for q, device in targets.items():
            copies.append(
                pltpu.make_async_remote_copy(
                    src_ref=send.at[step, pl.ds(SLOT * q, SLOT)],
                    dst_ref=recv.at[step, pl.ds(SLOT * (3 - q), SLOT)],
                    send_sem=send_sem.at[step, q],
                    recv_sem=recv_sem.at[step, q],
                    device_id=device,
                    device_id_type=MESH,
                )
            )
            copies[-1].start()
        return copies

    def arrived(step, copies):
        for copy in copies:
            copy.wait_recv()
        return nn(fq[...], recv[step])

    loads["tok"].wait()
    to_rows(tok, x)
    loads["g1"].wait()
    hat, rs_one = norm_parts(x[...])
    hat_one[...] = hat
    normed = (hat * g1[...]).astype(BF)
    loads["w1"].wait()
    packed_one[...] = nn(normed, w1[...]).astype(BF)

    for name in ("lab", "tq", "fq", "cot"):
        loads[name].wait()
    token = lax.broadcasted_iota(jnp.int32, (WT, WLON), 0)
    column = lax.broadcasted_iota(jnp.int32, (WT, WLON), 1)
    labelled = jnp.zeros((WT, WLON), F32)
    for b in range(WLAT):
        line_pair = lab[b].astype(F32)
        for a in range(LEV):
            line = jnp.broadcast_to(line_pair[a : a + 1, :], (WT, WLON))
            labelled = jnp.where(token - (a * WLAT + b) * WLON == column, line, labelled)
    label_col = jnp.sum(labelled, axis=-1, keepdims=True)
    label_rows = nn(tq[...], jnp.broadcast_to(label_col, (WT, LANES)).astype(BF)).astype(BF)
    lab_send[...] = label_rows
    lab_recv[pl.ds(3 * SLOT, SLOT)] = label_rows[:SLOT]
    to_rows(cot, ct)
    pl.semaphore_wait(barrier, len(around))
    lab_copies = []
    for q, device in owner_target.items():
        lab_copies.append(
            pltpu.make_async_remote_copy(
                src_ref=lab_send.at[pl.ds(SLOT * q, SLOT)],
                dst_ref=lab_recv.at[pl.ds(SLOT * (3 - q), SLOT)],
                send_sem=lab_send_sem.at[q],
                recv_sem=lab_recv_sem.at[q],
                device_id=device,
                device_id_type=MESH,
            )
        )
        lab_copies[-1].start()
    cot_copies = start(0, owner_target, ct[...].astype(BF))

    loads["b1"].wait()
    attention(packed_one, b1, probs_one, heads_one, None, masks)
    loads["wo1"].wait()
    mid_copies = start(1, owner_target, (x[...] + nn(heads_one[...], wo1[...])).astype(BF))

    ct[...] = arrived(0, cot_copies)
    loads["wdn"].wait()
    dh_keep[...] = nt(ct[...].astype(BF), wdn[...]).astype(BF)
    for copy in lab_copies:
        copy.wait_recv()
    label_here = nn(fq[...], lab_recv[...])
    row = lax.broadcasted_iota(jnp.int32, (WT, LANES), 0)
    late_row = jnp.logical_or(
        jnp.logical_and(row >= PLANE // 2, row < PLANE), row >= PLANE + PLANE // 2
    )
    edge = jnp.where(i == 0, 1.0, 0.0).astype(F32)
    ids = label_here * 2.0 + jnp.where(late_row, edge, 0.0)
    lane = lax.broadcasted_iota(jnp.int32, (WT, LANES), 1).astype(F32)
    one_hot = jnp.where(ids == lane, 1.0, 0.0).astype(BF)
    allowed_ref[...] = nt(one_hot, one_hot)
    for name in ("g2", "w2", "b2", "wo2", "g3", "wup"):
        loads[name].wait()

    mid = arrived(1, mid_copies)
    hat, rs_two = norm_parts(mid)
    hat_two[...] = hat
    packed_two[...] = nn((hat * g2[...]).astype(BF), w2[...]).astype(BF)
    attention(packed_two, b2, probs_two, heads_two, allowed_ref[...], masks)
    late = mid + nn(heads_two[...], wo2[...])

    hat, rs_three = norm_parts(late)
    u = nn((hat * g3[...]).astype(BF), wup[...])
    root = (2.0 / np.pi) ** 0.5
    square = u * u
    bent = jnp.tanh(root * u * (1.0 + 0.044715 * square))
    slope = 0.5 * (1.0 + bent) + (0.5 * root) * u * (1.0 - bent * bent) * (
        1.0 + (3.0 * 0.044715) * square
    )
    du = (dh_keep[...].astype(F32) * slope).astype(BF)
    hidden[...] = (0.5 * u * (1.0 + bent)).astype(BF)
    dn = nt(du, wup[...]).astype(BF).astype(F32)
    d_late = ct[...] + norm_back(hat, rs_three, g3[...], dn)

    d_heads[...] = nt(d_late.astype(BF), wo2[...]).astype(BF)
    attention_back(packed_two, probs_two, heads_two, d_heads, d_packed, masks)
    dn = nt(d_packed[...], w2[...]).astype(BF).astype(F32)
    d_mid = d_late + norm_back(hat_two[...], rs_two, g2[...], dn)
    back_copies = start(2, window_target, d_mid.astype(BF))
    out_copies = start(3, window_target, (late + nn(hidden[...], wdn[...])).astype(BF))

    d_mid = arrived(2, back_copies)
    d_heads[...] = nt(d_mid.astype(BF), wo1[...]).astype(BF)
    attention_back(packed_one, probs_one, heads_one, d_heads, d_packed, masks)
    to_cells(arrived(3, out_copies), out_stage)
    out_copy = pltpu.make_async_copy(out_stage, outputs, out_sem.at[0])
    out_copy.start()
    dn = nt(d_packed[...], w1[...]).astype(BF).astype(F32)
    to_cells(d_mid + norm_back(hat_one[...], rs_one, g1[...], dn), grad_stage)
    grad_copy = pltpu.make_async_copy(grad_stage, input_grad, out_sem.at[1])
    grad_copy.start()
    for copy in lab_copies + cot_copies + mid_copies + back_copies + out_copies:
        copy.wait_send()
    out_copy.wait()
    grad_copy.wait()


def write_out(first, second, first_out, second_out):
    first_out[...] = first[...]
    second_out[...] = second[...]


def per_device(n_lat, n_lon, *args):
    (tokens, labels, g1, w1, wo1, b1, g2, w2, wo2, b2, g3, wup, wdn, cot) = args
    place = quadrant_matrix()
    to_quad = jnp.asarray(place, BF)
    from_quad = jnp.asarray(place.T, BF)
    def cells(a):
        return a.transpose(1, 2, 0, 3).reshape(PLANE, LEV, D)

    operands = (
        cells(tokens), labels.transpose(1, 0, 2), g1.reshape(1, D), w1, wo1, b1, g2.reshape(1, D), w2, wo2, b2,
        g3.reshape(1, D), wup, wdn, cells(cot), to_quad, from_quad,
    )
    vm = pltpu.VMEM
    landing = [vm(a.shape, a.dtype) for a in operands]
    block = (PLANE, LEV, D)
    scratch = landing + [
        vm((WT, D), F32), vm((WT, D), F32),
        vm((WT, 3 * D), BF), vm((WT, 3 * D), BF),
        vm((HEADS * WT, WT), BF), vm((HEADS * WT, WT), BF),
        vm((WT, D), BF), vm((WT, D), BF), vm((WT, D), BF), vm((WT, 3 * D), BF),
        vm((WT, D), F32), vm((WT, D), F32), vm((WT, FF), BF), vm((WT, FF), BF), vm((WT, WT), F32),
        vm(block, BF), vm(block, BF),
        vm((4, ROWS, D), BF), vm((4, ROWS, D), BF), vm((ROWS, LANES), BF), vm((ROWS, LANES), BF),
        pltpu.SemaphoreType.DMA((len(operands),)),
        pltpu.SemaphoreType.DMA((4, 4)), pltpu.SemaphoreType.DMA((4, 4)),
        pltpu.SemaphoreType.DMA((4,)), pltpu.SemaphoreType.DMA((4,)),
        pltpu.SemaphoreType.DMA((2,)),
    ]
    whole = pl.BlockSpec(memory_space=pl.ANY)
    results = pl.pallas_call(
        functools.partial(kernel, n_lat, n_lon),
        out_shape=(jax.ShapeDtypeStruct(block, BF), jax.ShapeDtypeStruct(block, BF)),
        in_specs=[whole] * len(operands),
        out_specs=(whole, whole),
        scratch_shapes=scratch,
        compiler_params=pltpu.CompilerParams(
            collective_id=0, has_side_effects=True, vmem_limit_bytes=56 * 1024 * 1024
        ),
    )(*operands)
    results = pl.pallas_call(
        write_out,
        out_shape=(jax.ShapeDtypeStruct(block, BF), jax.ShapeDtypeStruct(block, BF)),
        in_specs=[pl.BlockSpec(memory_space=pltpu.VMEM)] * 2,
        out_specs=[pl.BlockSpec(memory_space=pltpu.VMEM)] * 2,
    )(*results)
    return tuple(a.reshape(WLAT, WLON, LEV, D).transpose(2, 0, 1, 3) for a in results)


def solution(mesh):
    field = P(None, "lat", "lon", None)
    return jax.shard_map(
        functools.partial(per_device, mesh.shape["lat"], mesh.shape["lon"]),
        mesh=mesh,
        in_specs=(field, P(None, "lat", "lon")) + (P(),) * 11 + (field,),
        out_specs=(field, field),
        check_vma=False,
    )
```

```python
import functools

import jax
import jax.numpy as jnp
import numpy as np
from jax import lax
from jax.experimental import pallas as pl
from jax.experimental.pallas import tpu as pltpu
from jax.sharding import PartitionSpec as P

MESH = pl.DeviceIdType.MESH
BF = jnp.bfloat16
F32 = jnp.float32

WLAT = 6
WLON = 12
LEV = 2
PLANE = WLAT * WLON
WT = LEV * PLANE
QUAD = WT // 4
SLOT = 48
ROWS = 4 * SLOT
D = 512
FF = 2048
CHUNK = 256
HEADS = 16
HD = D // HEADS
LANES = 128
PER = LANES // HD
GROUPS = D // LANES
SCALE = HD ** (-0.5)
EPSILON = 1e-05
LOG2E = 1.4426950408889634
TILE = 16


def quadrant_matrix():
    place = np.zeros((ROWS, WT), np.float32)
    hl, hc = WLAT // 2, WLON // 2
    for half_row in range(2):
        for half_col in range(2):
            for i in range(QUAD):
                level, r, c = i // (hl * hc), i // hc % hl, i % hc
                token = level * WLAT * WLON + (half_row * hl + r) * WLON + half_col * hc + c
                first = SLOT * (2 * half_row + half_col) + i
                for row in [first] if i < 32 else range(first, first + 16, 4):
                    place[row, token] = 1.0
    return place


def nn(a, b):
    return lax.dot_general(a, b, (((1,), (0,)), ((), ())), preferred_element_type=F32)


def nt(a, b):
    return lax.dot_general(a, b, (((1,), (1,)), ((), ())), preferred_element_type=F32)


def tn(a, b):
    return lax.dot_general(a, b, (((0,), (0,)), ((), ())), preferred_element_type=F32)


def norm_parts(x):
    centred = x - jnp.mean(x, axis=-1, keepdims=True)
    rs = lax.rsqrt(jnp.mean(centred * centred, axis=-1, keepdims=True) + EPSILON)
    return centred * rs, rs


def norm_back(hat, rs, gain, dy):
    t = dy * gain
    return rs * (
        t - jnp.mean(t, axis=-1, keepdims=True) - hat * jnp.mean(t * hat, axis=-1, keepdims=True)
    )


def head_masks():
    lane = lax.broadcasted_iota(jnp.int32, (WT, LANES), 1)
    return [jnp.logical_and(lane >= HD * j, lane < HD * (j + 1)) for j in range(PER)]


def pick(stack, masks):
    out = stack[:WT]
    for j in range(1, PER):
        out = jnp.where(masks[j], stack[WT * j : WT * (j + 1)], out)
    return out


def spread(group, masks):
    zero = jnp.zeros_like(group)
    return jnp.concatenate([jnp.where(m, group, zero) for m in masks], axis=0)


def group(packed, g):
    return [packed[:, D * n + LANES * g : D * n + LANES * (g + 1)] for n in range(3)]


def attention(packed, weight_of, probs, heads, inverse, masks):
    def score(g):
        q, k, _ = group(packed, g)
        return nt(spread(q, masks), k)

    ahead = score(0)
    for g in range(GROUPS):
        s = ahead
        if g + 1 < GROUPS:
            ahead = score(g + 1)
        v = group(packed, g)[2]
        parts = []
        for j in range(PER):
            h = PER * g + j
            parts.append(weight_of(s[WT * j : WT * (j + 1)], h).astype(BF))
            probs[pl.ds(WT * h, WT), :] = parts[-1]
        o = nn(jnp.concatenate(parts, axis=0), jnp.concatenate([v, jnp.ones_like(v)], axis=1))
        inv = 1.0 / pick(o[:, LANES:], masks)
        heads[:, LANES * g : LANES * (g + 1)] = (pick(o[:, :LANES], masks) * inv).astype(BF)
        inverse[:, LANES * g : LANES * (g + 1)] = inv


def attention_back(packed, probs, heads, inverse, d_heads, d_packed, masks):
    def first(g):
        lanes = slice(LANES * g, LANES * (g + 1))
        v = group(packed, g)[2]
        do = d_heads[:, lanes].astype(F32) * inverse[:, lanes]
        less = (-(do * heads[:, lanes].astype(F32))).astype(BF)
        do = spread(do.astype(BF), masks)
        left = jnp.concatenate([do, spread(less, masks)], axis=1)
        return do, nt(left, jnp.concatenate([v, jnp.ones_like(v)], axis=1))

    ahead = [first(0), first(1)]
    for g in range(GROUPS):
        do, dp = ahead.pop(0)
        if g + 2 < GROUPS:
            ahead.append(first(g + 2))
        q, k, _ = group(packed, g)
        p = probs[pl.ds(WT * PER * g, WT * PER), :]
        dv = tn(p, do)
        ds = (p.astype(F32) * dp).astype(BF)
        dk = tn(ds, spread(q, masks)) * SCALE
        dq = pick(nn(ds, k), masks) * SCALE
        for n, part in enumerate((dq, dk, dv)):
            d_packed[:, D * n + LANES * g : D * n + LANES * (g + 1)] = part.astype(BF)


def feed_gradient(normed, up, up_t, half_dh, hidden):
    root = (2.0 / np.pi) ** 0.5

    def lift(c):
        return nn(normed, up[:, CHUNK * c : CHUNK * (c + 1)])

    total = None
    ahead = lift(0)
    for c in range(FF // CHUNK):
        u = ahead
        if c + 1 < FF // CHUNK:
            ahead = lift(c + 1)
        lanes = slice(CHUNK * c, CHUNK * (c + 1))
        cubic = (u * u) * (root * 0.044715)
        bent = jnp.tanh(u * (cubic + root))
        above = 1.0 + bent
        slope = above * (1.0 + (u * (3.0 * cubic + root)) * (1.0 - bent))
        hidden[:, lanes] = (0.5 * u * above).astype(BF)
        part = nn((half_dh[:, lanes].astype(F32) * slope).astype(BF), up_t[lanes, :])
        total = part if total is None else total + part
    return total


def kernel(
    n_lat, n_lon,
    tokens, labels, gain_one, project_one, output_one, bias_one, gain_two, project_two, output_two,
    bias_two, gain_three, up_weight, down_weight, cotangent, to_quad, from_quad,
    outputs, input_grad,
    tok, lab, g1, w1, wo1, b1, g2, w2, wo2, b2, g3, wup, wdn, cot, tq, fq,
    x, ct, packed_one, packed_two, probs_one, probs_two, heads_one, heads_two, d_heads, d_packed,
    hat_one, hat_two, inv_one, inv_two, hidden, dh_keep, table_two, w1t, wo1t, w2t, wo2t, wupt,
    out_stage, grad_stage,
    send, recv, lab_send, lab_recv,
    load_sem, send_sem, recv_sem, lab_send_sem, lab_recv_sem, out_sem,
):
    i = lax.axis_index("lat")
    j = lax.axis_index("lon")
    north, south = lax.rem(i + n_lat - 1, n_lat), lax.rem(i + 1, n_lat)
    west, east = lax.rem(j + n_lon - 1, n_lon), lax.rem(j + 1, n_lon)
    barrier = pltpu.get_barrier_semaphore()
    around = [(i, east), (south, j), (south, east), (i, west), (north, j), (north, west)]
    for device in around:
        pl.semaphore_signal(barrier, inc=1, device_id=device, device_id_type=MESH)

    pairs = {
        "tok": (tokens, tok), "g1": (gain_one, g1), "w1": (project_one, w1), "b1": (bias_one, b1),
        "lab": (labels, lab), "tq": (to_quad, tq), "fq": (from_quad, fq),
        "wo1": (output_one, wo1), "g2": (gain_two, g2), "cot": (cotangent, cot), "w2": (project_two, w2),
        "wdn": (down_weight, wdn), "b2": (bias_two, b2),
        "wo2": (output_two, wo2), "g3": (gain_three, g3), "wup": (up_weight, wup),
    }
    loads = {}
    for at, (name, (source, target)) in enumerate(pairs.items()):
        loads[name] = pltpu.make_async_copy(source, target, load_sem.at[at])
        loads[name].start()

    masks = head_masks()

    def to_rows(source, target):
        for level in range(LEV):
            target[pl.ds(PLANE * level, PLANE), :] = source[:, level, :].astype(F32)

    def to_cells(value, target):
        for level in range(LEV):
            target[:, level, :] = value[PLANE * level : PLANE * (level + 1)].astype(BF)

    owner_target = {3: (south, east), 1: (i, east), 2: (south, j)}
    window_target = {0: (north, west), 2: (i, west), 1: (north, j)}

    quarter = lax.broadcasted_iota(jnp.int32, (TILE, LANES), 0)
    quarters = [
        jnp.logical_and(quarter >= 4 * k, quarter < 4 * (k + 1)) for k in range(GROUPS)
    ]

    def pack(target, rows):
        for a in range(2):
            for k in range(GROUPS):
                target[4 * a + k] = rows[TILE * a : TILE * (a + 1), LANES * k : LANES * (k + 1)]
        rest = rows[2 * TILE : SLOT]
        last = rest[:, :LANES]
        for k in range(1, GROUPS):
            last = jnp.where(quarters[k], rest[:, LANES * k : LANES * (k + 1)], last)
        target[8] = last

    def unpack(source):
        rows = [
            jnp.concatenate([source[4 * a + k] for k in range(GROUPS)], axis=1) for a in range(2)
        ]
        last = source[8]
        zero = jnp.zeros_like(last)
        rows.append(jnp.concatenate([jnp.where(m, last, zero) for m in quarters], axis=1))
        return jnp.concatenate(rows, axis=0)

    def start(step, targets, value):
        rows = nn(tq[...], value).astype(BF)
        copies = []
        for q, device in targets.items():
            pack(send.at[step, q], rows[SLOT * q : SLOT * (q + 1)])
            copies.append(
                pltpu.make_async_remote_copy(
                    src_ref=send.at[step, q],
                    dst_ref=recv.at[step, 3 - q],
                    send_sem=send_sem.at[step, q],
                    recv_sem=recv_sem.at[step, q],
                    device_id=device,
                    device_id_type=MESH,
                )
            )
            copies[-1].start()
        stay = 0 if targets is owner_target else 3
        pack(recv.at[step, 3 - stay], rows[SLOT * stay : SLOT * (stay + 1)])
        return copies

    def arrived(step, copies):
        for copy in copies:
            copy.wait_recv()
        return nn(fq[...], jnp.concatenate([unpack(recv.at[step, q]) for q in range(4)], axis=0))

    loads["tok"].wait()
    to_rows(tok, x)
    loads["g1"].wait()
    hat, rs_one = norm_parts(x[...])
    hat_one[...] = hat
    normed = (hat * g1[...]).astype(BF)
    loads["w1"].wait()
    packed_one[...] = nn(normed, w1[...]).astype(BF)

    for name in ("lab", "tq", "fq", "cot"):
        loads[name].wait()
    token = lax.broadcasted_iota(jnp.int32, (WT, WLON), 0)
    column = lax.broadcasted_iota(jnp.int32, (WT, WLON), 1)
    labelled = jnp.zeros((WT, WLON), F32)
    for b in range(WLAT):
        line_pair = lab[b].astype(F32)
        for a in range(LEV):
            line = jnp.broadcast_to(line_pair[a : a + 1, :], (WT, WLON))
            labelled = jnp.where(token - (a * WLAT + b) * WLON == column, line, labelled)
    label_col = jnp.sum(labelled, axis=-1, keepdims=True)
    label_rows = nn(tq[...], jnp.broadcast_to(label_col, (WT, LANES)).astype(BF))
    row = lax.broadcasted_iota(jnp.int32, (ROWS, LANES), 0)
    for q in range(4):
        spare = jnp.logical_and(row >= SLOT * q + QUAD, row < SLOT * (q + 1))
        label_rows = jnp.where(spare, 0.0, label_rows)
    label_rows = label_rows.astype(BF)
    lab_send[...] = label_rows
    lab_recv[pl.ds(3 * SLOT, SLOT)] = label_rows[:SLOT]
    to_rows(cot, ct)
    pl.semaphore_wait(barrier, len(around))
    lab_copies = []
    for q, device in owner_target.items():
        lab_copies.append(
            pltpu.make_async_remote_copy(
                src_ref=lab_send.at[pl.ds(SLOT * q, SLOT)],
                dst_ref=lab_recv.at[pl.ds(SLOT * (3 - q), SLOT)],
                send_sem=lab_send_sem.at[q],
                recv_sem=lab_recv_sem.at[q],
                device_id=device,
                device_id_type=MESH,
            )
        )
        lab_copies[-1].start()
    cot_copies = start(0, owner_target, ct[...].astype(BF))

    loads["b1"].wait()

    def weight_one(score, h):
        t = score * SCALE + b1[h].astype(F32)
        return jnp.exp(t - jnp.max(t, axis=-1, keepdims=True))

    def weight_two(score, h):
        t = score * (SCALE * LOG2E) + table_two[h]
        return jnp.exp2(t - jnp.max(t, axis=-1, keepdims=True))

    attention(packed_one, weight_one, probs_one, heads_one, inv_one, masks)
    loads["wo1"].wait()
    mid_copies = start(1, owner_target, (x[...] + nn(heads_one[...], wo1[...])).astype(BF))

    ct[...] = arrived(0, cot_copies)
    loads["wdn"].wait()
    dh_keep[...] = (0.5 * nt(ct[...].astype(BF), wdn[...])).astype(BF)
    for copy in lab_copies:
        copy.wait_recv()
    label_here = nn(fq[...], lab_recv[...])
    row = lax.broadcasted_iota(jnp.int32, (WT, LANES), 0)
    late_row = jnp.logical_or(
        jnp.logical_and(row >= PLANE // 2, row < PLANE), row >= PLANE + PLANE // 2
    )
    edge = jnp.where(i == 0, 1.0, 0.0).astype(F32)
    ids = label_here * 2.0 + jnp.where(late_row, edge, 0.0)
    lane = lax.broadcasted_iota(jnp.int32, (WT, LANES), 1).astype(F32)
    one_hot = jnp.where(ids == lane, 1.0, 0.0).astype(BF)
    barred = (nt(one_hot, one_hot) - 1.0) * 1e30
    loads["b2"].wait()
    for h in range(HEADS):
        table_two[h] = b2[h].astype(F32) * LOG2E + barred
    for name in ("g2", "w2", "wo2", "g3", "wup"):
        loads[name].wait()
    for weight, turned in ((wup, wupt), (w2, w2t), (wo2, wo2t), (w1, w1t), (wo1, wo1t)):
        turned[...] = weight[...].T

    mid = arrived(1, mid_copies)
    hat, rs_two = norm_parts(mid)
    hat_two[...] = hat
    packed_two[...] = nn((hat * g2[...]).astype(BF), w2[...]).astype(BF)
    attention(packed_two, weight_two, probs_two, heads_two, inv_two, masks)
    late = mid + nn(heads_two[...], wo2[...])

    hat, rs_three = norm_parts(late)
    normed = (hat * g3[...]).astype(BF)
    dn = feed_gradient(normed, wup, wupt, dh_keep, hidden).astype(BF).astype(F32)
    d_late = ct[...] + norm_back(hat, rs_three, g3[...], dn)

    d_heads[...] = nn(d_late.astype(BF), wo2t[...]).astype(BF)
    attention_back(packed_two, probs_two, heads_two, inv_two, d_heads, d_packed, masks)
    dn = nn(d_packed[...], w2t[...]).astype(BF).astype(F32)
    d_mid = d_late + norm_back(hat_two[...], rs_two, g2[...], dn)
    back_copies = start(2, window_target, d_mid.astype(BF))
    out_copies = start(3, window_target, (late + nn(hidden[...], wdn[...])).astype(BF))

    d_mid = arrived(2, back_copies)
    d_heads[...] = nn(d_mid.astype(BF), wo1t[...]).astype(BF)
    attention_back(packed_one, probs_one, heads_one, inv_one, d_heads, d_packed, masks)
    to_cells(arrived(3, out_copies), out_stage)
    out_copy = pltpu.make_async_copy(out_stage, outputs, out_sem.at[0])
    out_copy.start()
    dn = nn(d_packed[...], w1t[...]).astype(BF).astype(F32)
    to_cells(d_mid + norm_back(hat_one[...], rs_one, g1[...], dn), grad_stage)
    grad_copy = pltpu.make_async_copy(grad_stage, input_grad, out_sem.at[1])
    grad_copy.start()
    for copy in lab_copies + cot_copies + mid_copies + back_copies + out_copies:
        copy.wait_send()
    out_copy.wait()
    grad_copy.wait()


def write_out(first, second, first_out, second_out):
    first_out[...] = first[...]
    second_out[...] = second[...]


def per_device(n_lat, n_lon, *args):
    (tokens, labels, g1, w1, wo1, b1, g2, w2, wo2, b2, g3, wup, wdn, cot) = args
    place = quadrant_matrix()
    to_quad = jnp.asarray(place, BF)
    from_quad = jnp.asarray(place.T, BF)
    def cells(a):
        return a.transpose(1, 2, 0, 3).reshape(PLANE, LEV, D)

    operands = (
        cells(tokens), labels.transpose(1, 0, 2), g1.reshape(1, D), w1, wo1, b1, g2.reshape(1, D), w2, wo2, b2,
        g3.reshape(1, D), wup, wdn, cells(cot), to_quad, from_quad,
    )
    vm = pltpu.VMEM
    landing = [vm(a.shape, a.dtype) for a in operands]
    block = (PLANE, LEV, D)
    scratch = landing + [
        vm((WT, D), F32), vm((WT, D), F32),
        vm((WT, 3 * D), BF), vm((WT, 3 * D), BF),
        vm((HEADS * WT, WT), BF), vm((HEADS * WT, WT), BF),
        vm((WT, D), BF), vm((WT, D), BF), vm((WT, D), BF), vm((WT, 3 * D), BF),
        vm((WT, D), F32), vm((WT, D), F32), vm((WT, D), F32), vm((WT, D), F32),
        vm((WT, FF), BF), vm((WT, FF), BF), vm((HEADS, WT, WT), F32),
        vm((3 * D, D), BF), vm((D, D), BF), vm((3 * D, D), BF), vm((D, D), BF), vm((FF, D), BF),
        vm(block, BF), vm(block, BF),
        vm((4, 4, 9, TILE, LANES), BF), vm((4, 4, 9, TILE, LANES), BF), vm((ROWS, LANES), BF), vm((ROWS, LANES), BF),
        pltpu.SemaphoreType.DMA((len(operands),)),
        pltpu.SemaphoreType.DMA((4, 4)), pltpu.SemaphoreType.DMA((4, 4)),
        pltpu.SemaphoreType.DMA((4,)), pltpu.SemaphoreType.DMA((4,)),
        pltpu.SemaphoreType.DMA((2,)),
    ]
    whole = pl.BlockSpec(memory_space=pl.ANY)
    results = pl.pallas_call(
        functools.partial(kernel, n_lat, n_lon),
        out_shape=(jax.ShapeDtypeStruct(block, BF), jax.ShapeDtypeStruct(block, BF)),
        in_specs=[whole] * len(operands),
        out_specs=(whole, whole),
        scratch_shapes=scratch,
        compiler_params=pltpu.CompilerParams(
            collective_id=0, has_side_effects=True, vmem_limit_bytes=56 * 1024 * 1024
        ),
    )(*operands)
    results = pl.pallas_call(
        write_out,
        out_shape=(jax.ShapeDtypeStruct(block, BF), jax.ShapeDtypeStruct(block, BF)),
        in_specs=[pl.BlockSpec(memory_space=pltpu.VMEM)] * 2,
        out_specs=[pl.BlockSpec(memory_space=pltpu.VMEM)] * 2,
    )(*results)
    return tuple(a.reshape(WLAT, WLON, LEV, D).transpose(2, 0, 1, 3) for a in results)


def solution(mesh):
    field = P(None, "lat", "lon", None)
    return jax.shard_map(
        functools.partial(per_device, mesh.shape["lat"], mesh.shape["lon"]),
        mesh=mesh,
        in_specs=(field, P(None, "lat", "lon")) + (P(),) * 11 + (field,),
        out_specs=(field, field),
        check_vma=False,
    )
```

```python
import functools

import jax
import jax.numpy as jnp
import numpy as np
from jax import lax
from jax.experimental import pallas as pl
from jax.experimental.pallas import tpu as pltpu
from jax.sharding import PartitionSpec as P

MESH = pl.DeviceIdType.MESH
BF = jnp.bfloat16
F32 = jnp.float32

WLAT = 6
WLON = 12
LEV = 2
PLANE = WLAT * WLON
WT = LEV * PLANE
QUAD = WT // 4
SLOT = 48
ROWS = 4 * SLOT
D = 512
FF = 2048
CHUNK = 256
HEADS = 16
HD = D // HEADS
LANES = 128
PER = LANES // HD
GROUPS = D // LANES
SCALE = HD ** (-0.5)
EPSILON = 1e-05
LOG2E = 1.4426950408889634
TILE = 16


def quadrant_matrix():
    place = np.zeros((ROWS, WT), np.float32)
    hl, hc = WLAT // 2, WLON // 2
    for half_row in range(2):
        for half_col in range(2):
            for i in range(QUAD):
                level, r, c = i // (hl * hc), i // hc % hl, i % hc
                token = level * WLAT * WLON + (half_row * hl + r) * WLON + half_col * hc + c
                first = SLOT * (2 * half_row + half_col) + i
                for row in [first] if i < 32 else range(first, first + 16, 4):
                    place[row, token] = 1.0
    return place


def nn(a, b):
    return lax.dot_general(a, b, (((1,), (0,)), ((), ())), preferred_element_type=F32)


def nt(a, b):
    return lax.dot_general(a, b, (((1,), (1,)), ((), ())), preferred_element_type=F32)


def tn(a, b):
    return lax.dot_general(a, b, (((0,), (0,)), ((), ())), preferred_element_type=F32)


def norm_parts(x):
    centred = x - jnp.mean(x, axis=-1, keepdims=True)
    rs = lax.rsqrt(jnp.mean(centred * centred, axis=-1, keepdims=True) + EPSILON)
    return centred * rs, rs


def norm_back(hat, rs, gain, dy):
    t = dy * gain
    return rs * (
        t - jnp.mean(t, axis=-1, keepdims=True) - hat * jnp.mean(t * hat, axis=-1, keepdims=True)
    )


def head_masks():
    lane = lax.broadcasted_iota(jnp.int32, (WT, LANES), 1)
    return [jnp.logical_and(lane >= HD * j, lane < HD * (j + 1)) for j in range(PER)]


def pick(stack, masks):
    out = stack[:WT]
    for j in range(1, PER):
        out = jnp.where(masks[j], stack[WT * j : WT * (j + 1)], out)
    return out


def spread(group, masks):
    zero = jnp.zeros_like(group)
    return jnp.concatenate([jnp.where(m, group, zero) for m in masks], axis=0)


def group(packed, g):
    return [packed[:, D * n + LANES * g : D * n + LANES * (g + 1)] for n in range(3)]


def attention(packed, weight_of, probs, heads, inverse, masks):
    def score(g):
        q, k, _ = group(packed, g)
        return nt(spread(q, masks), k)

    ahead = score(0)
    for g in range(GROUPS):
        s = ahead
        if g + 1 < GROUPS:
            ahead = score(g + 1)
        v = group(packed, g)[2]
        parts = []
        for j in range(PER):
            h = PER * g + j
            parts.append(weight_of(s[WT * j : WT * (j + 1)], h).astype(BF))
            probs[pl.ds(WT * h, WT), :] = parts[-1]
        o = nn(jnp.concatenate(parts, axis=0), jnp.concatenate([v, jnp.ones_like(v)], axis=1))
        inv = 1.0 / pick(o[:, LANES:], masks)
        heads[:, LANES * g : LANES * (g + 1)] = (pick(o[:, :LANES], masks) * inv).astype(BF)
        inverse[:, LANES * g : LANES * (g + 1)] = inv


def attention_back(packed, probs, heads, inverse, d_heads, d_packed, masks):
    def first(g):
        lanes = slice(LANES * g, LANES * (g + 1))
        v = group(packed, g)[2]
        do = d_heads[:, lanes].astype(F32) * inverse[:, lanes]
        less = (-(do * heads[:, lanes].astype(F32))).astype(BF)
        do = spread(do.astype(BF), masks)
        left = jnp.concatenate([do, spread(less, masks)], axis=1)
        return do, nt(left, jnp.concatenate([v, jnp.ones_like(v)], axis=1))

    ahead = [first(0), first(1)]
    for g in range(GROUPS):
        do, dp = ahead.pop(0)
        if g + 2 < GROUPS:
            ahead.append(first(g + 2))
        q, k, _ = group(packed, g)
        p = probs[pl.ds(WT * PER * g, WT * PER), :]
        dv = tn(p, do)
        ds = (p.astype(F32) * dp).astype(BF)
        dk = tn(ds, spread(q, masks)) * SCALE
        dq = pick(nn(ds, k), masks) * SCALE
        for n, part in enumerate((dq, dk, dv)):
            d_packed[:, D * n + LANES * g : D * n + LANES * (g + 1)] = part.astype(BF)


def feed_gradient(normed, up, up_t, half_dh, hidden):
    root = (2.0 / np.pi) ** 0.5

    def lift(c):
        return nn(normed, up[:, CHUNK * c : CHUNK * (c + 1)])

    total = None
    ahead = lift(0)
    for c in range(FF // CHUNK):
        u = ahead
        if c + 1 < FF // CHUNK:
            ahead = lift(c + 1)
        lanes = slice(CHUNK * c, CHUNK * (c + 1))
        cubic = (u * u) * (root * 0.044715)
        bent = jnp.tanh(u * (cubic + root))
        above = 1.0 + bent
        slope = above * (1.0 + (u * (3.0 * cubic + root)) * (1.0 - bent))
        hidden[:, lanes] = (0.5 * u * above).astype(BF)
        part = nn((half_dh[:, lanes].astype(F32) * slope).astype(BF), up_t[lanes, :])
        total = part if total is None else total + part
    return total


def kernel(
    n_lat, n_lon,
    tokens, labels, gain_one, project_one, output_one, bias_one, gain_two, project_two, output_two,
    bias_two, gain_three, up_weight, down_weight, cotangent, to_quad, from_quad,
    outputs, input_grad,
    tok, lab, g1, w1, wo1, b1, g2, w2, wo2, b2, g3, wup, wdn, cot, tq, fq,
    x, ct, packed_one, packed_two, probs_one, probs_two, heads_one, heads_two, d_heads, d_packed,
    hat_one, hat_two, inv_one, inv_two, hidden, dh_keep, table_two, w1t, wo1t, w2t, wo2t, wupt,
    out_stage, grad_stage,
    send, recv, first_send, first_recv,
    load_sem, send_sem, recv_sem, out_sem,
):
    i = lax.axis_index("lat")
    j = lax.axis_index("lon")
    north, south = lax.rem(i + n_lat - 1, n_lat), lax.rem(i + 1, n_lat)
    west, east = lax.rem(j + n_lon - 1, n_lon), lax.rem(j + 1, n_lon)
    barrier = pltpu.get_barrier_semaphore()
    around = [(i, east), (south, j), (south, east), (i, west), (north, j), (north, west)]
    for device in around:
        pl.semaphore_signal(barrier, inc=1, device_id=device, device_id_type=MESH)

    pairs = {
        "tok": (tokens, tok), "g1": (gain_one, g1), "w1": (project_one, w1),
        "tq": (to_quad, tq), "cot": (cotangent, cot), "lab": (labels, lab),
        "b1": (bias_one, b1), "wo1": (output_one, wo1),
        "wup": (up_weight, wup), "w2": (project_two, w2), "wo2": (output_two, wo2),
        "fq": (from_quad, fq), "wdn": (down_weight, wdn), "b2": (bias_two, b2),
        "g2": (gain_two, g2), "g3": (gain_three, g3),
    }
    loads = {
        name: pltpu.make_async_copy(source, target, load_sem.at[at])
        for at, (name, (source, target)) in enumerate(pairs.items())
    }
    ordered = list(loads.values())
    for load in ordered[:8]:
        load.start()

    masks = head_masks()

    def to_rows(source, target):
        for level in range(LEV):
            target[pl.ds(PLANE * level, PLANE), :] = source[:, level, :].astype(F32)

    def to_cells(value, target):
        for level in range(LEV):
            target[:, level, :] = value[PLANE * level : PLANE * (level + 1)].astype(BF)

    owner_target = {3: (south, east), 1: (i, east), 2: (south, j)}
    window_target = {0: (north, west), 2: (i, west), 1: (north, j)}

    quarter = lax.broadcasted_iota(jnp.int32, (TILE, LANES), 0)
    quarters = [
        jnp.logical_and(quarter >= 4 * k, quarter < 4 * (k + 1)) for k in range(GROUPS)
    ]

    def pack(target, rows):
        for a in range(2):
            for k in range(GROUPS):
                target[4 * a + k] = rows[TILE * a : TILE * (a + 1), LANES * k : LANES * (k + 1)]
        rest = rows[2 * TILE : SLOT]
        last = rest[:, :LANES]
        for k in range(1, GROUPS):
            last = jnp.where(quarters[k], rest[:, LANES * k : LANES * (k + 1)], last)
        target[8] = last

    def add(target, rows, q):
        for a in range(3):
            target[9 + a] = rows[SLOT * q + TILE * a : SLOT * q + TILE * (a + 1)]

    def unpack(source):
        rows = [
            jnp.concatenate([source[4 * a + k] for k in range(GROUPS)], axis=1) for a in range(2)
        ]
        last = source[8]
        zero = jnp.zeros_like(last)
        rows.append(jnp.concatenate([jnp.where(m, last, zero) for m in quarters], axis=1))
        return jnp.concatenate(rows, axis=0)

    def start(step, targets, value, extra=None):
        rows = nn(tq[...], value).astype(BF)
        copies = []
        for q, device in targets.items():
            if extra is None:
                source, target = (send.at[step, q], recv.at[step, 3 - q])
            else:
                source, target = (first_send.at[q], first_recv.at[3 - q])
                add(source, extra, q)
            pack(source, rows[SLOT * q : SLOT * (q + 1)])
            copies.append(
                pltpu.make_async_remote_copy(
                    src_ref=source,
                    dst_ref=target,
                    send_sem=send_sem.at[step, q],
                    recv_sem=recv_sem.at[step, q],
                    device_id=device,
                    device_id_type=MESH,
                )
            )
            copies[-1].start()
        stay = 0 if targets is owner_target else 3
        if extra is None:
            target = recv.at[step, 3 - stay]
        else:
            target = first_recv.at[3 - stay]
            add(target, extra, stay)
        pack(target, rows[SLOT * stay : SLOT * (stay + 1)])
        return copies

    def arrived(step, copies):
        for copy in copies:
            copy.wait_recv()
        blocks = first_recv if step == 0 else recv.at[step]
        return nn(fq[...], jnp.concatenate([unpack(blocks.at[q]) for q in range(4)], axis=0))

    loads["tok"].wait()
    to_rows(tok, x)
    loads["g1"].wait()
    hat, rs_one = norm_parts(x[...])
    hat_one[...] = hat
    normed = (hat * g1[...]).astype(BF)

    for name in ("lab", "tq", "cot"):
        loads[name].wait()
    token = lax.broadcasted_iota(jnp.int32, (WT, WLON), 0)
    column = lax.broadcasted_iota(jnp.int32, (WT, WLON), 1)
    labelled = jnp.zeros((WT, WLON), F32)
    for b in range(WLAT):
        line_pair = lab[b].astype(F32)
        for a in range(LEV):
            line = jnp.broadcast_to(line_pair[a : a + 1, :], (WT, WLON))
            labelled = jnp.where(token - (a * WLAT + b) * WLON == column, line, labelled)
    label_col = jnp.sum(labelled, axis=-1, keepdims=True)
    label_rows = nn(tq[...], jnp.broadcast_to(label_col, (WT, LANES)).astype(BF))
    row = lax.broadcasted_iota(jnp.int32, (ROWS, LANES), 0)
    for q in range(4):
        spare = jnp.logical_and(row >= SLOT * q + QUAD, row < SLOT * (q + 1))
        label_rows = jnp.where(spare, 0.0, label_rows)
    label_rows = label_rows.astype(BF)
    to_rows(cot, ct)
    loads["w1"].wait()
    packed_one[...] = nn(normed, w1[...]).astype(BF)
    for load in ordered[8:]:
        load.start()
    pl.semaphore_wait(barrier, len(around))
    cot_copies = start(0, owner_target, ct[...].astype(BF), label_rows)
    loads["b1"].wait()

    def weight_one(score, h):
        t = score * SCALE + b1[h].astype(F32)
        return jnp.exp(t - jnp.max(t, axis=-1, keepdims=True))

    def weight_two(score, h):
        t = score * (SCALE * LOG2E) + table_two[h]
        return jnp.exp2(t - jnp.max(t, axis=-1, keepdims=True))

    attention(packed_one, weight_one, probs_one, heads_one, inv_one, masks)
    loads["wo1"].wait()
    mid_copies = start(1, owner_target, (x[...] + nn(heads_one[...], wo1[...])).astype(BF))

    for name in ("wup", "w2", "wo2", "fq"):
        loads[name].wait()
    for weight, turned in ((wup, wupt), (w2, w2t), (wo2, wo2t)):
        turned[...] = weight[...].T
    ct[...] = arrived(0, cot_copies)
    loads["wdn"].wait()
    dh_keep[...] = (0.5 * nt(ct[...].astype(BF), wdn[...])).astype(BF)
    label_rows = [first_recv[q, 9 + a] for q in range(4) for a in range(3)]
    label_here = nn(fq[...], jnp.concatenate(label_rows, axis=0))
    row = lax.broadcasted_iota(jnp.int32, (WT, LANES), 0)
    late_row = jnp.logical_or(
        jnp.logical_and(row >= PLANE // 2, row < PLANE), row >= PLANE + PLANE // 2
    )
    edge = jnp.where(i == 0, 1.0, 0.0).astype(F32)
    ids = label_here * 2.0 + jnp.where(late_row, edge, 0.0)
    lane = lax.broadcasted_iota(jnp.int32, (WT, LANES), 1).astype(F32)
    one_hot = jnp.where(ids == lane, 1.0, 0.0).astype(BF)
    barred = (nt(one_hot, one_hot) - 1.0) * 1e30
    loads["b2"].wait()
    for h in range(HEADS):
        table_two[h] = b2[h].astype(F32) * LOG2E + barred
    for name in ("g2", "g3"):
        loads[name].wait()

    mid = arrived(1, mid_copies)
    hat, rs_two = norm_parts(mid)
    hat_two[...] = hat
    packed_two[...] = nn((hat * g2[...]).astype(BF), w2[...]).astype(BF)
    attention(packed_two, weight_two, probs_two, heads_two, inv_two, masks)
    late = mid + nn(heads_two[...], wo2[...])

    hat, rs_three = norm_parts(late)
    normed = (hat * g3[...]).astype(BF)
    dn = feed_gradient(normed, wup, wupt, dh_keep, hidden).astype(BF).astype(F32)
    d_late = ct[...] + norm_back(hat, rs_three, g3[...], dn)

    d_heads[...] = nn(d_late.astype(BF), wo2t[...]).astype(BF)
    attention_back(packed_two, probs_two, heads_two, inv_two, d_heads, d_packed, masks)
    dn = nn(d_packed[...], w2t[...]).astype(BF).astype(F32)
    d_mid = d_late + norm_back(hat_two[...], rs_two, g2[...], dn)
    back_copies = start(2, window_target, d_mid.astype(BF))
    out_copies = start(3, window_target, (late + nn(hidden[...], wdn[...])).astype(BF))

    for weight, turned in ((wo1, wo1t), (w1, w1t)):
        turned[...] = weight[...].T

    d_mid = arrived(2, back_copies)
    d_heads[...] = nn(d_mid.astype(BF), wo1t[...]).astype(BF)
    attention_back(packed_one, probs_one, heads_one, inv_one, d_heads, d_packed, masks)
    to_cells(arrived(3, out_copies), out_stage)
    out_copy = pltpu.make_async_copy(out_stage, outputs, out_sem.at[0])
    out_copy.start()
    dn = nn(d_packed[...], w1t[...]).astype(BF).astype(F32)
    to_cells(d_mid + norm_back(hat_one[...], rs_one, g1[...], dn), grad_stage)
    grad_copy = pltpu.make_async_copy(grad_stage, input_grad, out_sem.at[1])
    grad_copy.start()
    for copy in cot_copies + mid_copies + back_copies + out_copies:
        copy.wait_send()
    out_copy.wait()
    grad_copy.wait()


def write_out(first, second, first_out, second_out):
    first_out[...] = first[...]
    second_out[...] = second[...]


def per_device(n_lat, n_lon, *args):
    (tokens, labels, g1, w1, wo1, b1, g2, w2, wo2, b2, g3, wup, wdn, cot) = args
    place = quadrant_matrix()
    to_quad = jnp.asarray(place, BF)
    from_quad = jnp.asarray(place.T, BF)
    def cells(a):
        return a.transpose(1, 2, 0, 3).reshape(PLANE, LEV, D)

    operands = (
        cells(tokens), labels.transpose(1, 0, 2), g1.reshape(1, D), w1, wo1, b1, g2.reshape(1, D), w2, wo2, b2,
        g3.reshape(1, D), wup, wdn, cells(cot), to_quad, from_quad,
    )
    vm = pltpu.VMEM
    landing = [vm(a.shape, a.dtype) for a in operands]
    block = (PLANE, LEV, D)
    scratch = landing + [
        vm((WT, D), F32), vm((WT, D), F32),
        vm((WT, 3 * D), BF), vm((WT, 3 * D), BF),
        vm((HEADS * WT, WT), BF), vm((HEADS * WT, WT), BF),
        vm((WT, D), BF), vm((WT, D), BF), vm((WT, D), BF), vm((WT, 3 * D), BF),
        vm((WT, D), F32), vm((WT, D), F32), vm((WT, D), F32), vm((WT, D), F32),
        vm((WT, FF), BF), vm((WT, FF), BF), vm((HEADS, WT, WT), F32),
        vm((3 * D, D), BF), vm((D, D), BF), vm((3 * D, D), BF), vm((D, D), BF), vm((FF, D), BF),
        vm(block, BF), vm(block, BF),
        vm((4, 4, 9, TILE, LANES), BF), vm((4, 4, 9, TILE, LANES), BF),
        vm((4, 12, TILE, LANES), BF), vm((4, 12, TILE, LANES), BF),
        pltpu.SemaphoreType.DMA((len(operands),)),
        pltpu.SemaphoreType.DMA((4, 4)), pltpu.SemaphoreType.DMA((4, 4)),
        pltpu.SemaphoreType.DMA((2,)),
    ]
    whole = pl.BlockSpec(memory_space=pl.ANY)
    results = pl.pallas_call(
        functools.partial(kernel, n_lat, n_lon),
        out_shape=(jax.ShapeDtypeStruct(block, BF), jax.ShapeDtypeStruct(block, BF)),
        in_specs=[whole] * len(operands),
        out_specs=(whole, whole),
        scratch_shapes=scratch,
        compiler_params=pltpu.CompilerParams(
            collective_id=0, has_side_effects=True, vmem_limit_bytes=56 * 1024 * 1024
        ),
    )(*operands)
    results = pl.pallas_call(
        write_out,
        out_shape=(jax.ShapeDtypeStruct(block, BF), jax.ShapeDtypeStruct(block, BF)),
        in_specs=[pl.BlockSpec(memory_space=pltpu.VMEM)] * 2,
        out_specs=[pl.BlockSpec(memory_space=pltpu.VMEM)] * 2,
    )(*results)
    return tuple(a.reshape(WLAT, WLON, LEV, D).transpose(2, 0, 1, 3) for a in results)


def solution(mesh):
    field = P(None, "lat", "lon", None)
    return jax.shard_map(
        functools.partial(per_device, mesh.shape["lat"], mesh.shape["lon"]),
        mesh=mesh,
        in_specs=(field, P(None, "lat", "lon")) + (P(),) * 11 + (field,),
        out_specs=(field, field),
        check_vma=False,
    )
```

```python
import functools

import jax
import jax.numpy as jnp
import numpy as np
from jax import lax
from jax.experimental import pallas as pl
from jax.experimental.pallas import tpu as pltpu
from jax.sharding import PartitionSpec as P

MESH = pl.DeviceIdType.MESH
BF = jnp.bfloat16
F32 = jnp.float32

WLAT = 6
WLON = 12
LEV = 2
PLANE = WLAT * WLON
WT = LEV * PLANE
QUAD = WT // 4
SLOT = 48
ROWS = 4 * SLOT
D = 512
FF = 2048
CHUNK = 256
HEADS = 16
HD = D // HEADS
LANES = 128
PER = LANES // HD
GROUPS = D // LANES
SCALE = HD ** (-0.5)
EPSILON = 1e-05
LOG2E = 1.4426950408889634
TILE = 16


def quadrant_matrix():
    place = np.zeros((ROWS, WT), np.float32)
    hl, hc = WLAT // 2, WLON // 2
    for half_row in range(2):
        for half_col in range(2):
            for i in range(QUAD):
                level, r, c = i // (hl * hc), i // hc % hl, i % hc
                token = level * WLAT * WLON + (half_row * hl + r) * WLON + half_col * hc + c
                first = SLOT * (2 * half_row + half_col) + i
                for row in [first] if i < 32 else range(first, first + 16, 4):
                    place[row, token] = 1.0
    return place


def nn(a, b):
    return lax.dot_general(a, b, (((1,), (0,)), ((), ())), preferred_element_type=F32)


def nt(a, b):
    return lax.dot_general(a, b, (((1,), (1,)), ((), ())), preferred_element_type=F32)


def tn(a, b):
    return lax.dot_general(a, b, (((0,), (0,)), ((), ())), preferred_element_type=F32)


def norm_parts(x):
    centred = x - jnp.mean(x, axis=-1, keepdims=True)
    rs = lax.rsqrt(jnp.mean(centred * centred, axis=-1, keepdims=True) + EPSILON)
    return centred * rs, rs


def norm_back(hat, rs, gain, dy):
    t = dy * gain
    return rs * (
        t - jnp.mean(t, axis=-1, keepdims=True) - hat * jnp.mean(t * hat, axis=-1, keepdims=True)
    )


def head_masks():
    lane = lax.broadcasted_iota(jnp.int32, (WT, LANES), 1)
    return [jnp.logical_and(lane >= HD * j, lane < HD * (j + 1)) for j in range(PER)]


def pick(stack, masks):
    out = stack[:WT]
    for j in range(1, PER):
        out = jnp.where(masks[j], stack[WT * j : WT * (j + 1)], out)
    return out


def spread(group, masks):
    zero = jnp.zeros_like(group)
    return jnp.concatenate([jnp.where(m, group, zero) for m in masks], axis=0)


def group(packed, g):
    return [packed[:, D * n + LANES * g : D * n + LANES * (g + 1)] for n in range(3)]


def attention(packed, weight_of, probs, heads, inverse, masks):
    def score(g):
        q, k, _ = group(packed, g)
        return nt(spread(q, masks), k)

    ahead = score(0)
    for g in range(GROUPS):
        s = ahead
        if g + 1 < GROUPS:
            ahead = score(g + 1)
        v = group(packed, g)[2]
        parts = []
        for j in range(PER):
            h = PER * g + j
            parts.append(weight_of(s[WT * j : WT * (j + 1)], h).astype(BF))
            probs[pl.ds(WT * h, WT), :] = parts[-1]
        o = nn(jnp.concatenate(parts, axis=0), jnp.concatenate([v, jnp.ones_like(v)], axis=1))
        inv = 1.0 / pick(o[:, LANES:], masks)
        heads[:, LANES * g : LANES * (g + 1)] = (pick(o[:, :LANES], masks) * inv).astype(BF)
        inverse[:, LANES * g : LANES * (g + 1)] = inv


def attention_back(packed, probs, heads, inverse, d_heads, d_packed, masks):
    def first(g):
        lanes = slice(LANES * g, LANES * (g + 1))
        v = group(packed, g)[2]
        do = d_heads[:, lanes].astype(F32) * inverse[:, lanes]
        less = (-(do * heads[:, lanes].astype(F32))).astype(BF)
        do = spread(do.astype(BF), masks)
        left = jnp.concatenate([do, spread(less, masks)], axis=1)
        return do, nt(left, jnp.concatenate([v, jnp.ones_like(v)], axis=1))

    ahead = [first(0), first(1)]
    for g in range(GROUPS):
        do, dp = ahead.pop(0)
        if g + 2 < GROUPS:
            ahead.append(first(g + 2))
        q, k, _ = group(packed, g)
        p = probs[pl.ds(WT * PER * g, WT * PER), :]
        dv = tn(p, do)
        ds = (p.astype(F32) * dp).astype(BF)
        dk = tn(ds, spread(q, masks)) * SCALE
        dq = pick(nn(ds, k), masks) * SCALE
        for n, part in enumerate((dq, dk, dv)):
            d_packed[:, D * n + LANES * g : D * n + LANES * (g + 1)] = part.astype(BF)


def feed_gradient(normed, up, up_t, half_dh, hidden):
    root = (2.0 / np.pi) ** 0.5

    def lift(c):
        return nn(normed, up[:, CHUNK * c : CHUNK * (c + 1)])

    total = None
    ahead = lift(0)
    for c in range(FF // CHUNK):
        u = ahead
        if c + 1 < FF // CHUNK:
            ahead = lift(c + 1)
        lanes = slice(CHUNK * c, CHUNK * (c + 1))
        cubic = (u * u) * (root * 0.044715)
        bent = jnp.tanh(u * (cubic + root))
        above = 1.0 + bent
        slope = above * (1.0 + (u * (3.0 * cubic + root)) * (1.0 - bent))
        hidden[:, lanes] = (0.5 * u * above).astype(BF)
        part = nn((half_dh[:, lanes].astype(F32) * slope).astype(BF), up_t[lanes, :])
        total = part if total is None else total + part
    return total


def kernel(
    n_lat, n_lon,
    tokens, labels, gain_one, project_one, output_one, bias_one, gain_two, project_two, output_two,
    bias_two, gain_three, up_weight, down_weight, cotangent, to_quad, from_quad,
    outputs, input_grad,
    tok, lab, g1, w1, wo1, b1, g2, w2, wo2, b2, g3, wup, wdn, cot, tq, fq,
    x, ct, packed_one, packed_two, probs_one, probs_two, heads_one, heads_two, d_heads, d_packed,
    hat_one, hat_two, inv_one, inv_two, hidden, dh_keep, table_two, w1t, wo1t, w2t, wo2t, wupt,
    send, recv, first_send, first_recv,
    load_sem, send_sem, recv_sem,
):
    i = lax.axis_index("lat")
    j = lax.axis_index("lon")
    north, south = lax.rem(i + n_lat - 1, n_lat), lax.rem(i + 1, n_lat)
    west, east = lax.rem(j + n_lon - 1, n_lon), lax.rem(j + 1, n_lon)
    barrier = pltpu.get_barrier_semaphore()
    around = [(i, east), (south, j), (south, east), (i, west), (north, j), (north, west)]
    for device in around:
        pl.semaphore_signal(barrier, inc=1, device_id=device, device_id_type=MESH)

    pairs = {
        "tok": (tokens, tok), "g1": (gain_one, g1), "lab": (labels, lab), "tq": (to_quad, tq),
        "cot": (cotangent, cot), "w1": (project_one, w1),
        "b1": (bias_one, b1), "wo1": (output_one, wo1),
        "wup": (up_weight, wup), "w2": (project_two, w2), "wo2": (output_two, wo2),
        "fq": (from_quad, fq), "wdn": (down_weight, wdn), "b2": (bias_two, b2),
        "g2": (gain_two, g2), "g3": (gain_three, g3),
    }
    loads = {
        name: pltpu.make_async_copy(source, target, load_sem.at[at])
        for at, (name, (source, target)) in enumerate(pairs.items())
    }
    ordered = list(loads.values())
    for load in ordered[:8]:
        load.start()

    masks = head_masks()

    def to_rows(source, target):
        for level in range(LEV):
            target[pl.ds(PLANE * level, PLANE), :] = source[:, level, :].astype(F32)

    def to_cells(value, target):
        for level in range(LEV):
            target[:, level, :] = value[PLANE * level : PLANE * (level + 1)].astype(BF)

    owner_target = {3: (south, east), 1: (i, east), 2: (south, j)}
    window_target = {1: (north, j), 0: (north, west), 2: (i, west)}

    quarter = lax.broadcasted_iota(jnp.int32, (TILE, LANES), 0)
    quarters = [
        jnp.logical_and(quarter >= 4 * k, quarter < 4 * (k + 1)) for k in range(GROUPS)
    ]

    def pack(target, rows):
        for a in range(2):
            for k in range(GROUPS):
                target[4 * a + k] = rows[TILE * a : TILE * (a + 1), LANES * k : LANES * (k + 1)]
        rest = rows[2 * TILE : SLOT]
        last = rest[:, :LANES]
        for k in range(1, GROUPS):
            last = jnp.where(quarters[k], rest[:, LANES * k : LANES * (k + 1)], last)
        target[8] = last

    def add(target, rows, q):
        for a in range(3):
            target[9 + a] = rows[SLOT * q + TILE * a : SLOT * q + TILE * (a + 1)]

    def unpack(source):
        rows = [
            jnp.concatenate([source[4 * a + k] for k in range(GROUPS)], axis=1) for a in range(2)
        ]
        last = source[8]
        zero = jnp.zeros_like(last)
        rows.append(jnp.concatenate([jnp.where(m, last, zero) for m in quarters], axis=1))
        return jnp.concatenate(rows, axis=0)

    def start(step, targets, value, extra=None):
        rows = nn(tq[...], value).astype(BF)
        copies = []
        for q, device in targets.items():
            if extra is None:
                source, target = (send.at[step, q], recv.at[step, 3 - q])
            else:
                source, target = (first_send.at[q], first_recv.at[3 - q])
                add(source, extra, q)
            pack(source, rows[SLOT * q : SLOT * (q + 1)])
            copies.append(
                pltpu.make_async_remote_copy(
                    src_ref=source,
                    dst_ref=target,
                    send_sem=send_sem.at[step, q],
                    recv_sem=recv_sem.at[step, q],
                    device_id=device,
                    device_id_type=MESH,
                )
            )
            copies[-1].start()
        stay = 0 if targets is owner_target else 3
        if extra is None:
            target = recv.at[step, 3 - stay]
        else:
            target = first_recv.at[3 - stay]
            add(target, extra, stay)
        pack(target, rows[SLOT * stay : SLOT * (stay + 1)])
        return copies

    def arrived(step, copies):
        for copy in copies:
            copy.wait_recv()
        blocks = first_recv if step == 0 else recv.at[step]
        return nn(fq[...], jnp.concatenate([unpack(blocks.at[q]) for q in range(4)], axis=0))

    loads["tok"].wait()
    to_rows(tok, x)
    loads["g1"].wait()
    hat, rs_one = norm_parts(x[...])
    hat_one[...] = hat
    normed = (hat * g1[...]).astype(BF)

    for name in ("lab", "tq", "cot"):
        loads[name].wait()
    token = lax.broadcasted_iota(jnp.int32, (WT, WLON), 0)
    column = lax.broadcasted_iota(jnp.int32, (WT, WLON), 1)
    labelled = jnp.zeros((WT, WLON), F32)
    for b in range(WLAT):
        line_pair = lab[b].astype(F32)
        for a in range(LEV):
            line = jnp.broadcast_to(line_pair[a : a + 1, :], (WT, WLON))
            labelled = jnp.where(token - (a * WLAT + b) * WLON == column, line, labelled)
    label_col = jnp.sum(labelled, axis=-1, keepdims=True)
    label_rows = nn(tq[...], jnp.broadcast_to(label_col, (WT, LANES)).astype(BF))
    row = lax.broadcasted_iota(jnp.int32, (ROWS, LANES), 0)
    for q in range(4):
        spare = jnp.logical_and(row >= SLOT * q + QUAD, row < SLOT * (q + 1))
        label_rows = jnp.where(spare, 0.0, label_rows)
    label_rows = label_rows.astype(BF)
    to_rows(cot, ct)
    loads["w1"].wait()
    packed_one[...] = nn(normed, w1[...]).astype(BF)
    for load in ordered[8:]:
        load.start()
    pl.semaphore_wait(barrier, len(around))
    cot_copies = start(0, owner_target, ct[...].astype(BF), label_rows)
    loads["b1"].wait()

    def weight_one(score, h):
        t = score * SCALE + b1[h].astype(F32)
        return jnp.exp(t - jnp.max(t, axis=-1, keepdims=True))

    def weight_two(score, h):
        t = score * (SCALE * LOG2E) + table_two[h]
        return jnp.exp2(t - jnp.max(t, axis=-1, keepdims=True))

    attention(packed_one, weight_one, probs_one, heads_one, inv_one, masks)
    loads["wo1"].wait()
    mid_copies = start(1, owner_target, (x[...] + nn(heads_one[...], wo1[...])).astype(BF))

    for name in ("wup", "w2", "wo2", "fq"):
        loads[name].wait()
    for weight, turned in ((wup, wupt), (w2, w2t), (wo2, wo2t)):
        turned[...] = weight[...].T
    ct[...] = arrived(0, cot_copies)
    loads["wdn"].wait()
    dh_keep[...] = (0.5 * nt(ct[...].astype(BF), wdn[...])).astype(BF)
    label_rows = [first_recv[q, 9 + a] for q in range(4) for a in range(3)]
    label_here = nn(fq[...], jnp.concatenate(label_rows, axis=0))
    row = lax.broadcasted_iota(jnp.int32, (WT, LANES), 0)
    late_row = jnp.logical_or(
        jnp.logical_and(row >= PLANE // 2, row < PLANE), row >= PLANE + PLANE // 2
    )
    edge = jnp.where(i == 0, 1.0, 0.0).astype(F32)
    ids = label_here * 2.0 + jnp.where(late_row, edge, 0.0)
    lane = lax.broadcasted_iota(jnp.int32, (WT, LANES), 1).astype(F32)
    one_hot = jnp.where(ids == lane, 1.0, 0.0).astype(BF)
    barred = (nt(one_hot, one_hot) - 1.0) * 1e30
    loads["b2"].wait()
    for h in range(HEADS):
        table_two[h] = b2[h].astype(F32) * LOG2E + barred
    for name in ("g2", "g3"):
        loads[name].wait()

    mid = arrived(1, mid_copies)
    hat, rs_two = norm_parts(mid)
    hat_two[...] = hat
    packed_two[...] = nn((hat * g2[...]).astype(BF), w2[...]).astype(BF)
    attention(packed_two, weight_two, probs_two, heads_two, inv_two, masks)
    late = mid + nn(heads_two[...], wo2[...])

    hat, rs_three = norm_parts(late)
    normed = (hat * g3[...]).astype(BF)
    dn = feed_gradient(normed, wup, wupt, dh_keep, hidden).astype(BF).astype(F32)
    d_late = ct[...] + norm_back(hat, rs_three, g3[...], dn)

    d_heads[...] = nn(d_late.astype(BF), wo2t[...]).astype(BF)
    attention_back(packed_two, probs_two, heads_two, inv_two, d_heads, d_packed, masks)
    dn = nn(d_packed[...], w2t[...]).astype(BF).astype(F32)
    d_mid = d_late + norm_back(hat_two[...], rs_two, g2[...], dn)
    back_copies = start(2, window_target, d_mid.astype(BF))
    out_copies = start(3, window_target, (late + nn(hidden[...], wdn[...])).astype(BF))

    for weight, turned in ((wo1, wo1t), (w1, w1t)):
        turned[...] = weight[...].T

    d_mid = arrived(2, back_copies)
    d_heads[...] = nn(d_mid.astype(BF), wo1t[...]).astype(BF)
    attention_back(packed_one, probs_one, heads_one, inv_one, d_heads, d_packed, masks)
    to_cells(arrived(3, out_copies), outputs)
    dn = nn(d_packed[...], w1t[...]).astype(BF).astype(F32)
    to_cells(d_mid + norm_back(hat_one[...], rs_one, g1[...], dn), input_grad)
    for copy in cot_copies + mid_copies + back_copies + out_copies:
        copy.wait_send()


def write_out(first, second, first_out, second_out):
    first_out[...] = first[...]
    second_out[...] = second[...]


def per_device(n_lat, n_lon, *args):
    (tokens, labels, g1, w1, wo1, b1, g2, w2, wo2, b2, g3, wup, wdn, cot) = args
    place = quadrant_matrix()
    to_quad = jnp.asarray(place, BF)
    from_quad = jnp.asarray(place.T, BF)
    def cells(a):
        return a.transpose(1, 2, 0, 3).reshape(PLANE, LEV, D)

    operands = (
        cells(tokens), labels.transpose(1, 0, 2), g1.reshape(1, D), w1, wo1, b1, g2.reshape(1, D), w2, wo2, b2,
        g3.reshape(1, D), wup, wdn, cells(cot), to_quad, from_quad,
    )
    vm = pltpu.VMEM
    landing = [vm(a.shape, a.dtype) for a in operands]
    block = (PLANE, LEV, D)
    scratch = landing + [
        vm((WT, D), F32), vm((WT, D), F32),
        vm((WT, 3 * D), BF), vm((WT, 3 * D), BF),
        vm((HEADS * WT, WT), BF), vm((HEADS * WT, WT), BF),
        vm((WT, D), BF), vm((WT, D), BF), vm((WT, D), BF), vm((WT, 3 * D), BF),
        vm((WT, D), F32), vm((WT, D), F32), vm((WT, D), F32), vm((WT, D), F32),
        vm((WT, FF), BF), vm((WT, FF), BF), vm((HEADS, WT, WT), F32),
        vm((3 * D, D), BF), vm((D, D), BF), vm((3 * D, D), BF), vm((D, D), BF), vm((FF, D), BF),
        vm((4, 4, 9, TILE, LANES), BF), vm((4, 4, 9, TILE, LANES), BF),
        vm((4, 12, TILE, LANES), BF), vm((4, 12, TILE, LANES), BF),
        pltpu.SemaphoreType.DMA((len(operands),)),
        pltpu.SemaphoreType.DMA((4, 4)), pltpu.SemaphoreType.DMA((4, 4)),
    ]
    whole = pl.BlockSpec(memory_space=pl.ANY)
    results = pl.pallas_call(
        functools.partial(kernel, n_lat, n_lon),
        out_shape=(pltpu.VMEM(block, BF), pltpu.VMEM(block, BF)),
        in_specs=[whole] * len(operands),
        out_specs=[pl.BlockSpec(memory_space=pltpu.VMEM)] * 2,
        scratch_shapes=scratch,
        compiler_params=pltpu.CompilerParams(
            collective_id=0, has_side_effects=True, vmem_limit_bytes=56 * 1024 * 1024
        ),
    )(*operands)
    results = [pltpu.with_memory_space_constraint(a, pltpu.VMEM) for a in results]
    results = pl.pallas_call(
        write_out,
        out_shape=(jax.ShapeDtypeStruct(block, BF), jax.ShapeDtypeStruct(block, BF)),
        in_specs=[pl.BlockSpec(memory_space=pltpu.VMEM)] * 2,
        out_specs=[pl.BlockSpec(memory_space=pltpu.VMEM)] * 2,
    )(*results)
    return tuple(a.reshape(WLAT, WLON, LEV, D).transpose(2, 0, 1, 3) for a in results)


def solution(mesh):
    field = P(None, "lat", "lon", None)
    return jax.shard_map(
        functools.partial(per_device, mesh.shape["lat"], mesh.shape["lon"]),
        mesh=mesh,
        in_specs=(field, P(None, "lat", "lon")) + (P(),) * 11 + (field,),
        out_specs=(field, field),
        check_vma=False,
    )
```

```python
import functools

import jax
import jax.numpy as jnp
import numpy as np
from jax import lax
from jax.experimental import pallas as pl
from jax.experimental.pallas import tpu as pltpu
from jax.sharding import PartitionSpec as P

MESH = pl.DeviceIdType.MESH
BF = jnp.bfloat16
F32 = jnp.float32

WLAT = 6
WLON = 12
LEV = 2
PLANE = WLAT * WLON
WT = LEV * PLANE
QUAD = WT // 4
SLOT = 48
ROWS = 4 * SLOT
D = 512
FF = 2048
CHUNK = 256
HEADS = 16
HD = D // HEADS
LANES = 128
PER = LANES // HD
GROUPS = D // LANES
SCALE = HD ** (-0.5)
EPSILON = 1e-05
LOG2E = 1.4426950408889634
TILE = 16


def quadrant_matrix():
    place = np.zeros((ROWS, WT), np.float32)
    hl, hc = WLAT // 2, WLON // 2
    for half_row in range(2):
        for half_col in range(2):
            for i in range(QUAD):
                level, r, c = i // (hl * hc), i // hc % hl, i % hc
                token = level * WLAT * WLON + (half_row * hl + r) * WLON + half_col * hc + c
                first = SLOT * (2 * half_row + half_col) + i
                for row in [first] if i < 32 else range(first, first + 16, 4):
                    place[row, token] = 1.0
    return place


def nn(a, b):
    return lax.dot_general(a, b, (((1,), (0,)), ((), ())), preferred_element_type=F32)


def nt(a, b):
    return lax.dot_general(a, b, (((1,), (1,)), ((), ())), preferred_element_type=F32)


def tn(a, b):
    return lax.dot_general(a, b, (((0,), (0,)), ((), ())), preferred_element_type=F32)


def norm_parts(x):
    centred = x - jnp.mean(x, axis=-1, keepdims=True)
    rs = lax.rsqrt(jnp.mean(centred * centred, axis=-1, keepdims=True) + EPSILON)
    return centred * rs, rs


def norm_back(hat, rs, gain, dy):
    t = dy * gain
    return rs * (
        t - jnp.mean(t, axis=-1, keepdims=True) - hat * jnp.mean(t * hat, axis=-1, keepdims=True)
    )


def head_masks():
    lane = lax.broadcasted_iota(jnp.int32, (WT, LANES), 1)
    return [jnp.logical_and(lane >= HD * j, lane < HD * (j + 1)) for j in range(PER)]


def pick(stack, masks):
    out = stack[:WT]
    for j in range(1, PER):
        out = jnp.where(masks[j], stack[WT * j : WT * (j + 1)], out)
    return out


def spread(group, masks):
    zero = jnp.zeros_like(group)
    return jnp.concatenate([jnp.where(m, group, zero) for m in masks], axis=0)


def group(packed, g):
    return [packed[:, D * n + LANES * g : D * n + LANES * (g + 1)] for n in range(3)]


def attention(packed, weight_of, probs, heads, inverse, masks):
    def score(g):
        q, k, _ = group(packed, g)
        return nt(spread(q, masks), k)

    ahead = score(0)
    for g in range(GROUPS):
        s = ahead
        if g + 1 < GROUPS:
            ahead = score(g + 1)
        v = group(packed, g)[2]
        parts = []
        for j in range(PER):
            h = PER * g + j
            parts.append(weight_of(s[WT * j : WT * (j + 1)], h).astype(BF))
            probs[pl.ds(WT * h, WT), :] = parts[-1]
        o = nn(jnp.concatenate(parts, axis=0), jnp.concatenate([v, jnp.ones_like(v)], axis=1))
        inv = 1.0 / pick(o[:, LANES:], masks)
        heads[:, LANES * g : LANES * (g + 1)] = (pick(o[:, :LANES], masks) * inv).astype(BF)
        inverse[:, LANES * g : LANES * (g + 1)] = inv


def attention_back(packed, probs, heads, inverse, d_heads, d_packed, masks):
    def first(g):
        lanes = slice(LANES * g, LANES * (g + 1))
        v = group(packed, g)[2]
        do = d_heads[:, lanes].astype(F32) * inverse[:, lanes]
        less = (-(do * heads[:, lanes].astype(F32))).astype(BF)
        do = spread(do.astype(BF), masks)
        left = jnp.concatenate([do, spread(less, masks)], axis=1)
        return do, nt(left, jnp.concatenate([v, jnp.ones_like(v)], axis=1))

    ahead = [first(0), first(1)]
    for g in range(GROUPS):
        do, dp = ahead.pop(0)
        if g + 2 < GROUPS:
            ahead.append(first(g + 2))
        q, k, _ = group(packed, g)
        p = probs[pl.ds(WT * PER * g, WT * PER), :]
        dv = tn(p, do)
        ds = (p.astype(F32) * dp).astype(BF)
        dk = tn(ds, spread(q, masks)) * SCALE
        dq = pick(nn(ds, k), masks) * SCALE
        for n, part in enumerate((dq, dk, dv)):
            d_packed[:, D * n + LANES * g : D * n + LANES * (g + 1)] = part.astype(BF)


def feed_gradient(normed, up, up_t, half_dh, hidden):
    root = (2.0 / np.pi) ** 0.5

    def lift(c):
        return nn(normed, up[:, CHUNK * c : CHUNK * (c + 1)])

    total = None
    ahead = lift(0)
    for c in range(FF // CHUNK):
        u = ahead
        if c + 1 < FF // CHUNK:
            ahead = lift(c + 1)
        lanes = slice(CHUNK * c, CHUNK * (c + 1))
        cubic = (u * u) * (root * 0.044715)
        bent = jnp.tanh(u * (cubic + root))
        above = 1.0 + bent
        slope = above * (1.0 + (u * (3.0 * cubic + root)) * (1.0 - bent))
        hidden[:, lanes] = (0.5 * u * above).astype(BF)
        part = nn((half_dh[:, lanes].astype(F32) * slope).astype(BF), up_t[lanes, :])
        total = part if total is None else total + part
    return total


def kernel(
    n_lat, n_lon,
    tokens, labels, gain_one, project_one, output_one, bias_one, gain_two, project_two, output_two,
    bias_two, gain_three, up_weight, down_weight, cotangent, to_quad, from_quad,
    outputs, input_grad,
    tok, lab, g1, w1, wo1, b1, g2, w2, wo2, b2, g3, wup, wdn, cot, tq, fq,
    x, ct, packed_one, packed_two, probs_one, probs_two, heads_one, heads_two, d_heads, d_packed,
    hat_one, hat_two, inv_one, inv_two, hidden, dh_keep, table_two, w1t, wo1t, w2t, wo2t, wupt,
    send, recv, first_send, first_recv,
    load_sem, send_sem, recv_sem,
):
    i = lax.axis_index("lat")
    j = lax.axis_index("lon")
    north, south = lax.rem(i + n_lat - 1, n_lat), lax.rem(i + 1, n_lat)
    west, east = lax.rem(j + n_lon - 1, n_lon), lax.rem(j + 1, n_lon)
    barrier = pltpu.get_barrier_semaphore()
    around = [(i, east), (south, j), (south, east), (i, west), (north, j), (north, west)]
    for device in around:
        pl.semaphore_signal(barrier, inc=1, device_id=device, device_id_type=MESH)

    pairs = {
        "tok": (tokens, tok), "g1": (gain_one, g1), "lab": (labels, lab), "tq": (to_quad, tq),
        "cot": (cotangent, cot), "w1": (project_one, w1),
        "b1": (bias_one, b1), "wo1": (output_one, wo1),
        "wup": (up_weight, wup), "w2": (project_two, w2), "wo2": (output_two, wo2),
        "fq": (from_quad, fq), "wdn": (down_weight, wdn), "b2": (bias_two, b2),
        "g2": (gain_two, g2), "g3": (gain_three, g3),
    }
    loads = {
        name: pltpu.make_async_copy(source, target, load_sem.at[at])
        for at, (name, (source, target)) in enumerate(pairs.items())
    }
    ordered = list(loads.values())
    for load in ordered[:8]:
        load.start()

    masks = head_masks()

    def to_rows(source, target):
        for level in range(LEV):
            target[pl.ds(PLANE * level, PLANE), :] = source[:, level, :].astype(F32)

    def to_cells(value, target):
        for level in range(LEV):
            target[:, level, :] = value[PLANE * level : PLANE * (level + 1)].astype(BF)

    owner_target = {3: (south, east), 1: (i, east), 2: (south, j)}
    window_target = {1: (north, j), 0: (north, west), 2: (i, west)}

    quarter = lax.broadcasted_iota(jnp.int32, (TILE, LANES), 0)
    quarters = [
        jnp.logical_and(quarter >= 4 * k, quarter < 4 * (k + 1)) for k in range(GROUPS)
    ]

    def pack(target, rows):
        for a in range(2):
            for k in range(GROUPS):
                target[4 * a + k] = rows[TILE * a : TILE * (a + 1), LANES * k : LANES * (k + 1)]
        rest = rows[2 * TILE : SLOT]
        last = rest[:, :LANES]
        for k in range(1, GROUPS):
            last = jnp.where(quarters[k], rest[:, LANES * k : LANES * (k + 1)], last)
        target[8] = last

    def add(target, rows, q):
        for a in range(3):
            target[9 + a] = rows[SLOT * q + TILE * a : SLOT * q + TILE * (a + 1)]

    def unpack(source):
        rows = [
            jnp.concatenate([source[4 * a + k] for k in range(GROUPS)], axis=1) for a in range(2)
        ]
        last = source[8]
        zero = jnp.zeros_like(last)
        rows.append(jnp.concatenate([jnp.where(m, last, zero) for m in quarters], axis=1))
        return jnp.concatenate(rows, axis=0)

    def start(step, targets, value, extra=None, go=True):
        rows = nn(tq[...], value).astype(BF)
        copies = []
        for q, device in targets.items():
            if extra is None:
                source, target = (send.at[step, q], recv.at[step, 3 - q])
            else:
                source, target = (first_send.at[q], first_recv.at[3 - q])
                add(source, extra, q)
            pack(source, rows[SLOT * q : SLOT * (q + 1)])
            copies.append(
                pltpu.make_async_remote_copy(
                    src_ref=source,
                    dst_ref=target,
                    send_sem=send_sem.at[step, q],
                    recv_sem=recv_sem.at[step, q],
                    device_id=device,
                    device_id_type=MESH,
                )
            )
            if go:
                copies[-1].start()
        stay = 0 if targets is owner_target else 3
        if extra is None:
            target = recv.at[step, 3 - stay]
        else:
            target = first_recv.at[3 - stay]
            add(target, extra, stay)
        pack(target, rows[SLOT * stay : SLOT * (stay + 1)])
        return copies

    def arrived(step, copies):
        for copy in copies:
            copy.wait_recv()
        blocks = first_recv if step == 0 else recv.at[step]
        return nn(fq[...], jnp.concatenate([unpack(blocks.at[q]) for q in range(4)], axis=0))

    loads["tok"].wait()
    to_rows(tok, x)
    loads["g1"].wait()
    hat, rs_one = norm_parts(x[...])
    hat_one[...] = hat
    normed = (hat * g1[...]).astype(BF)

    for name in ("lab", "tq", "cot"):
        loads[name].wait()
    token = lax.broadcasted_iota(jnp.int32, (WT, WLON), 0)
    column = lax.broadcasted_iota(jnp.int32, (WT, WLON), 1)
    labelled = jnp.zeros((WT, WLON), F32)
    for b in range(WLAT):
        line_pair = lab[b].astype(F32)
        for a in range(LEV):
            line = jnp.broadcast_to(line_pair[a : a + 1, :], (WT, WLON))
            labelled = jnp.where(token - (a * WLAT + b) * WLON == column, line, labelled)
    label_col = jnp.sum(labelled, axis=-1, keepdims=True)
    label_rows = nn(tq[...], jnp.broadcast_to(label_col, (WT, LANES)).astype(BF))
    row = lax.broadcasted_iota(jnp.int32, (ROWS, LANES), 0)
    for q in range(4):
        spare = jnp.logical_and(row >= SLOT * q + QUAD, row < SLOT * (q + 1))
        label_rows = jnp.where(spare, 0.0, label_rows)
    label_rows = label_rows.astype(BF)
    to_rows(cot, ct)
    cot_copies = start(0, owner_target, ct[...].astype(BF), label_rows, go=False)
    loads["w1"].wait()
    packed_one[...] = nn(normed, w1[...]).astype(BF)
    for load in ordered[8:]:
        load.start()
    pl.semaphore_wait(barrier, len(around))
    for copy in cot_copies:
        copy.start()
    loads["b1"].wait()

    def weight_one(score, h):
        t = score * SCALE + b1[h].astype(F32)
        return jnp.exp(t - jnp.max(t, axis=-1, keepdims=True))

    def weight_two(score, h):
        t = score * (SCALE * LOG2E) + table_two[h]
        return jnp.exp2(t - jnp.max(t, axis=-1, keepdims=True))

    attention(packed_one, weight_one, probs_one, heads_one, inv_one, masks)
    loads["wo1"].wait()
    mid_copies = start(1, owner_target, (x[...] + nn(heads_one[...], wo1[...])).astype(BF))

    for name in ("wup", "w2", "wo2", "fq"):
        loads[name].wait()
    for weight, turned in ((wup, wupt), (w2, w2t), (wo2, wo2t)):
        turned[...] = weight[...].T
    ct[...] = arrived(0, cot_copies)
    loads["wdn"].wait()
    dh_keep[...] = (0.5 * nt(ct[...].astype(BF), wdn[...])).astype(BF)
    label_rows = [first_recv[q, 9 + a] for q in range(4) for a in range(3)]
    label_here = nn(fq[...], jnp.concatenate(label_rows, axis=0))
    row = lax.broadcasted_iota(jnp.int32, (WT, LANES), 0)
    late_row = jnp.logical_or(
        jnp.logical_and(row >= PLANE // 2, row < PLANE), row >= PLANE + PLANE // 2
    )
    edge = jnp.where(i == 0, 1.0, 0.0).astype(F32)
    ids = label_here * 2.0 + jnp.where(late_row, edge, 0.0)
    lane = lax.broadcasted_iota(jnp.int32, (WT, LANES), 1).astype(F32)
    one_hot = jnp.where(ids == lane, 1.0, 0.0).astype(BF)
    barred = (nt(one_hot, one_hot) - 1.0) * 1e30
    loads["b2"].wait()
    for h in range(HEADS):
        table_two[h] = b2[h].astype(F32) * LOG2E + barred
    for name in ("g2", "g3"):
        loads[name].wait()

    mid = arrived(1, mid_copies)
    hat, rs_two = norm_parts(mid)
    hat_two[...] = hat
    packed_two[...] = nn((hat * g2[...]).astype(BF), w2[...]).astype(BF)
    attention(packed_two, weight_two, probs_two, heads_two, inv_two, masks)
    late = mid + nn(heads_two[...], wo2[...])

    hat, rs_three = norm_parts(late)
    normed = (hat * g3[...]).astype(BF)
    dn = feed_gradient(normed, wup, wupt, dh_keep, hidden).astype(BF).astype(F32)
    d_late = ct[...] + norm_back(hat, rs_three, g3[...], dn)

    d_heads[...] = nn(d_late.astype(BF), wo2t[...]).astype(BF)
    attention_back(packed_two, probs_two, heads_two, inv_two, d_heads, d_packed, masks)
    dn = nn(d_packed[...], w2t[...]).astype(BF).astype(F32)
    d_mid = d_late + norm_back(hat_two[...], rs_two, g2[...], dn)
    back_copies = start(2, window_target, d_mid.astype(BF))
    out_copies = start(3, window_target, (late + nn(hidden[...], wdn[...])).astype(BF))

    for weight, turned in ((wo1, wo1t), (w1, w1t)):
        turned[...] = weight[...].T

    d_mid = arrived(2, back_copies)
    d_heads[...] = nn(d_mid.astype(BF), wo1t[...]).astype(BF)
    attention_back(packed_one, probs_one, heads_one, inv_one, d_heads, d_packed, masks)
    to_cells(arrived(3, out_copies), outputs)
    dn = nn(d_packed[...], w1t[...]).astype(BF).astype(F32)
    to_cells(d_mid + norm_back(hat_one[...], rs_one, g1[...], dn), input_grad)
    for copy in cot_copies + mid_copies + back_copies + out_copies:
        copy.wait_send()


def write_out(first, second, first_out, second_out):
    first_out[...] = first[...]
    second_out[...] = second[...]


def per_device(n_lat, n_lon, *args):
    (tokens, labels, g1, w1, wo1, b1, g2, w2, wo2, b2, g3, wup, wdn, cot) = args
    place = quadrant_matrix()
    to_quad = jnp.asarray(place, BF)
    from_quad = jnp.asarray(place.T, BF)
    def cells(a):
        return a.transpose(1, 2, 0, 3).reshape(PLANE, LEV, D)

    operands = (
        cells(tokens), labels.transpose(1, 0, 2), g1.reshape(1, D), w1, wo1, b1, g2.reshape(1, D), w2, wo2, b2,
        g3.reshape(1, D), wup, wdn, cells(cot), to_quad, from_quad,
    )
    vm = pltpu.VMEM
    landing = [vm(a.shape, a.dtype) for a in operands]
    block = (PLANE, LEV, D)
    scratch = landing + [
        vm((WT, D), F32), vm((WT, D), F32),
        vm((WT, 3 * D), BF), vm((WT, 3 * D), BF),
        vm((HEADS * WT, WT), BF), vm((HEADS * WT, WT), BF),
        vm((WT, D), BF), vm((WT, D), BF), vm((WT, D), BF), vm((WT, 3 * D), BF),
        vm((WT, D), F32), vm((WT, D), F32), vm((WT, D), F32), vm((WT, D), F32),
        vm((WT, FF), BF), vm((WT, FF), BF), vm((HEADS, WT, WT), F32),
        vm((3 * D, D), BF), vm((D, D), BF), vm((3 * D, D), BF), vm((D, D), BF), vm((FF, D), BF),
        vm((4, 4, 9, TILE, LANES), BF), vm((4, 4, 9, TILE, LANES), BF),
        vm((4, 12, TILE, LANES), BF), vm((4, 12, TILE, LANES), BF),
        pltpu.SemaphoreType.DMA((len(operands),)),
        pltpu.SemaphoreType.DMA((4, 4)), pltpu.SemaphoreType.DMA((4, 4)),
    ]
    whole = pl.BlockSpec(memory_space=pl.ANY)
    results = pl.pallas_call(
        functools.partial(kernel, n_lat, n_lon),
        out_shape=(pltpu.VMEM(block, BF), pltpu.VMEM(block, BF)),
        in_specs=[whole] * len(operands),
        out_specs=[pl.BlockSpec(memory_space=pltpu.VMEM)] * 2,
        scratch_shapes=scratch,
        compiler_params=pltpu.CompilerParams(
            collective_id=0, has_side_effects=True, vmem_limit_bytes=56 * 1024 * 1024
        ),
    )(*operands)
    results = [pltpu.with_memory_space_constraint(a, pltpu.VMEM) for a in results]
    results = pl.pallas_call(
        write_out,
        out_shape=(jax.ShapeDtypeStruct(block, BF), jax.ShapeDtypeStruct(block, BF)),
        in_specs=[pl.BlockSpec(memory_space=pltpu.VMEM)] * 2,
        out_specs=[pl.BlockSpec(memory_space=pltpu.VMEM)] * 2,
    )(*results)
    return tuple(a.reshape(WLAT, WLON, LEV, D).transpose(2, 0, 1, 3) for a in results)


def solution(mesh):
    field = P(None, "lat", "lon", None)
    return jax.shard_map(
        functools.partial(per_device, mesh.shape["lat"], mesh.shape["lon"]),
        mesh=mesh,
        in_specs=(field, P(None, "lat", "lon")) + (P(),) * 11 + (field,),
        out_specs=(field, field),
        check_vma=False,
    )
```

```python
import functools

import jax
import jax.numpy as jnp
import numpy as np
from jax import lax
from jax.experimental import pallas as pl
from jax.experimental.pallas import tpu as pltpu
from jax.sharding import PartitionSpec as P

MESH = pl.DeviceIdType.MESH
BF = jnp.bfloat16
F32 = jnp.float32

WLAT = 6
WLON = 12
LEV = 2
PLANE = WLAT * WLON
WT = LEV * PLANE
QUAD = WT // 4
SLOT = 48
ROWS = 4 * SLOT
D = 512
FF = 2048
CHUNK = 256
HEADS = 16
HD = D // HEADS
LANES = 128
PER = LANES // HD
GROUPS = D // LANES
SCALE = HD ** (-0.5)
EPSILON = 1e-05
LOG2E = 1.4426950408889634
TILE = 16


def quadrant_matrix():
    place = np.zeros((ROWS, WT), np.float32)
    hl, hc = WLAT // 2, WLON // 2
    for half_row in range(2):
        for half_col in range(2):
            for i in range(QUAD):
                level, r, c = i // (hl * hc), i // hc % hl, i % hc
                token = level * WLAT * WLON + (half_row * hl + r) * WLON + half_col * hc + c
                first = SLOT * (2 * half_row + half_col) + i
                for row in [first] if i < 32 else range(first, first + 16, 4):
                    place[row, token] = 1.0
    return place


def nn(a, b):
    return lax.dot_general(a, b, (((1,), (0,)), ((), ())), preferred_element_type=F32)


def nt(a, b):
    return lax.dot_general(a, b, (((1,), (1,)), ((), ())), preferred_element_type=F32)


def tn(a, b):
    return lax.dot_general(a, b, (((0,), (0,)), ((), ())), preferred_element_type=F32)


def norm_parts(x):
    centred = x - jnp.mean(x, axis=-1, keepdims=True)
    rs = lax.rsqrt(jnp.mean(centred * centred, axis=-1, keepdims=True) + EPSILON)
    return centred * rs, rs


def norm_back(hat, rs, gain, dy):
    t = dy * gain
    return rs * (
        t - jnp.mean(t, axis=-1, keepdims=True) - hat * jnp.mean(t * hat, axis=-1, keepdims=True)
    )


def head_masks():
    lane = lax.broadcasted_iota(jnp.int32, (WT, LANES), 1)
    return [jnp.logical_and(lane >= HD * j, lane < HD * (j + 1)) for j in range(PER)]


def pick(stack, masks):
    out = stack[:WT]
    for j in range(1, PER):
        out = jnp.where(masks[j], stack[WT * j : WT * (j + 1)], out)
    return out


def spread(group, masks):
    zero = jnp.zeros_like(group)
    return jnp.concatenate([jnp.where(m, group, zero) for m in masks], axis=0)


def group(packed, g):
    return [packed[:, D * n + LANES * g : D * n + LANES * (g + 1)] for n in range(3)]


def attention(packed, weight_of, probs, heads, inverse, masks):
    def score(g):
        q, k, _ = group(packed, g)
        return nt(spread(q, masks), k)

    ahead = score(0)
    for g in range(GROUPS):
        s = ahead
        if g + 1 < GROUPS:
            ahead = score(g + 1)
        v = group(packed, g)[2]
        parts = []
        for j in range(PER):
            h = PER * g + j
            parts.append(weight_of(s[WT * j : WT * (j + 1)], h).astype(BF))
            probs[pl.ds(WT * h, WT), :] = parts[-1]
        o = nn(jnp.concatenate(parts, axis=0), jnp.concatenate([v, jnp.ones_like(v)], axis=1))
        inv = 1.0 / pick(o[:, LANES:], masks)
        heads[:, LANES * g : LANES * (g + 1)] = (pick(o[:, :LANES], masks) * inv).astype(BF)
        inverse[:, LANES * g : LANES * (g + 1)] = inv


def attention_back(packed, probs, heads, inverse, d_heads, d_packed, masks):
    def first(g):
        lanes = slice(LANES * g, LANES * (g + 1))
        v = group(packed, g)[2]
        do = d_heads[:, lanes].astype(F32) * inverse[:, lanes]
        less = (-(do * heads[:, lanes].astype(F32))).astype(BF)
        do = spread(do.astype(BF), masks)
        left = jnp.concatenate([do, spread(less, masks)], axis=1)
        return do, nt(left, jnp.concatenate([v, jnp.ones_like(v)], axis=1))

    ahead = [first(g) for g in range(GROUPS)]
    for g in range(GROUPS):
        do, dp = ahead.pop(0)
        q, k, _ = group(packed, g)
        p = probs[pl.ds(WT * PER * g, WT * PER), :]
        dv = tn(p, do)
        ds = (p.astype(F32) * dp).astype(BF)
        dk = tn(ds, spread(q, masks)) * SCALE
        dq = pick(nn(ds, k), masks) * SCALE
        for n, part in enumerate((dq, dk, dv)):
            d_packed[:, D * n + LANES * g : D * n + LANES * (g + 1)] = part.astype(BF)


def feed_gradient(normed, up, up_t, half_dh, hidden):
    root = (2.0 / np.pi) ** 0.5

    def lift(c):
        return nn(normed, up[:, CHUNK * c : CHUNK * (c + 1)])

    total = None
    ahead = lift(0)
    for c in range(FF // CHUNK):
        u = ahead
        if c + 1 < FF // CHUNK:
            ahead = lift(c + 1)
        lanes = slice(CHUNK * c, CHUNK * (c + 1))
        cubic = (u * u) * (root * 0.044715)
        bent = jnp.tanh(u * (cubic + root))
        above = 1.0 + bent
        slope = above * (1.0 + (u * (3.0 * cubic + root)) * (1.0 - bent))
        hidden[:, lanes] = (0.5 * u * above).astype(BF)
        part = nn((half_dh[:, lanes].astype(F32) * slope).astype(BF), up_t[lanes, :])
        total = part if total is None else total + part
    return total


def kernel(
    n_lat, n_lon,
    tokens, labels, gain_one, project_one, output_one, bias_one, gain_two, project_two, output_two,
    bias_two, gain_three, up_weight, down_weight, cotangent, to_quad, from_quad,
    outputs, input_grad,
    tok, lab, g1, w1, wo1, b1, g2, w2, wo2, b2, g3, wup, wdn, cot, tq, fq,
    x, ct, packed_one, packed_two, probs_one, probs_two, heads_one, heads_two, d_heads, d_packed,
    hat_one, hat_two, inv_one, inv_two, hidden, dh_keep, table_two, w1t, wo1t, w2t, wo2t, wupt,
    send, recv, first_send, first_recv,
    load_sem, send_sem, recv_sem,
):
    i = lax.axis_index("lat")
    j = lax.axis_index("lon")
    north, south = lax.rem(i + n_lat - 1, n_lat), lax.rem(i + 1, n_lat)
    west, east = lax.rem(j + n_lon - 1, n_lon), lax.rem(j + 1, n_lon)
    barrier = pltpu.get_barrier_semaphore()
    around = [(i, east), (south, j), (south, east), (i, west), (north, j), (north, west)]
    for device in around:
        pl.semaphore_signal(barrier, inc=1, device_id=device, device_id_type=MESH)

    pairs = {
        "tok": (tokens, tok), "g1": (gain_one, g1), "lab": (labels, lab), "tq": (to_quad, tq),
        "cot": (cotangent, cot), "w1": (project_one, w1),
        "b1": (bias_one, b1), "wo1": (output_one, wo1),
        "wup": (up_weight, wup), "w2": (project_two, w2), "wo2": (output_two, wo2),
        "fq": (from_quad, fq), "wdn": (down_weight, wdn), "b2": (bias_two, b2),
        "g2": (gain_two, g2), "g3": (gain_three, g3),
    }
    loads = {
        name: pltpu.make_async_copy(source, target, load_sem.at[at])
        for at, (name, (source, target)) in enumerate(pairs.items())
    }
    ordered = list(loads.values())
    for load in ordered[:8]:
        load.start()

    masks = head_masks()

    def to_rows(source, target):
        for level in range(LEV):
            target[pl.ds(PLANE * level, PLANE), :] = source[:, level, :].astype(F32)

    def to_cells(value, target):
        for level in range(LEV):
            target[:, level, :] = value[PLANE * level : PLANE * (level + 1)].astype(BF)

    owner_target = {3: (south, east), 1: (i, east), 2: (south, j)}
    window_target = {1: (north, j), 0: (north, west), 2: (i, west)}

    quarter = lax.broadcasted_iota(jnp.int32, (TILE, LANES), 0)
    quarters = [
        jnp.logical_and(quarter >= 4 * k, quarter < 4 * (k + 1)) for k in range(GROUPS)
    ]

    def pack(target, rows):
        for a in range(2):
            for k in range(GROUPS):
                target[4 * a + k] = rows[TILE * a : TILE * (a + 1), LANES * k : LANES * (k + 1)]
        rest = rows[2 * TILE : SLOT]
        last = rest[:, :LANES]
        for k in range(1, GROUPS):
            last = jnp.where(quarters[k], rest[:, LANES * k : LANES * (k + 1)], last)
        target[8] = last

    def add(target, rows, q):
        for a in range(3):
            target[9 + a] = rows[SLOT * q + TILE * a : SLOT * q + TILE * (a + 1)]

    def unpack(source):
        rows = [
            jnp.concatenate([source[4 * a + k] for k in range(GROUPS)], axis=1) for a in range(2)
        ]
        last = source[8]
        zero = jnp.zeros_like(last)
        rows.append(jnp.concatenate([jnp.where(m, last, zero) for m in quarters], axis=1))
        return jnp.concatenate(rows, axis=0)

    def start(step, targets, value, extra=None, go=True):
        rows = nn(tq[...], value).astype(BF)
        copies = []
        for q, device in targets.items():
            if extra is None:
                source, target = (send.at[step, q], recv.at[step, 3 - q])
            else:
                source, target = (first_send.at[q], first_recv.at[3 - q])
                add(source, extra, q)
            pack(source, rows[SLOT * q : SLOT * (q + 1)])
            copies.append(
                pltpu.make_async_remote_copy(
                    src_ref=source,
                    dst_ref=target,
                    send_sem=send_sem.at[step, q],
                    recv_sem=recv_sem.at[step, q],
                    device_id=device,
                    device_id_type=MESH,
                )
            )
            if go:
                copies[-1].start()
        stay = 0 if targets is owner_target else 3
        if extra is None:
            target = recv.at[step, 3 - stay]
        else:
            target = first_recv.at[3 - stay]
            add(target, extra, stay)
        pack(target, rows[SLOT * stay : SLOT * (stay + 1)])
        return copies

    def arrived(step, copies):
        for copy in copies:
            copy.wait_recv()
        blocks = first_recv if step == 0 else recv.at[step]
        return nn(fq[...], jnp.concatenate([unpack(blocks.at[q]) for q in range(4)], axis=0))

    loads["tok"].wait()
    to_rows(tok, x)
    loads["g1"].wait()
    hat, rs_one = norm_parts(x[...])
    hat_one[...] = hat
    normed = (hat * g1[...]).astype(BF)

    for name in ("lab", "tq", "cot"):
        loads[name].wait()
    token = lax.broadcasted_iota(jnp.int32, (WT, WLON), 0)
    column = lax.broadcasted_iota(jnp.int32, (WT, WLON), 1)
    labelled = jnp.zeros((WT, WLON), F32)
    for b in range(WLAT):
        line_pair = lab[b].astype(F32)
        for a in range(LEV):
            line = jnp.broadcast_to(line_pair[a : a + 1, :], (WT, WLON))
            labelled = jnp.where(token - (a * WLAT + b) * WLON == column, line, labelled)
    label_col = jnp.sum(labelled, axis=-1, keepdims=True)
    label_rows = nn(tq[...], jnp.broadcast_to(label_col, (WT, LANES)).astype(BF))
    row = lax.broadcasted_iota(jnp.int32, (ROWS, LANES), 0)
    for q in range(4):
        spare = jnp.logical_and(row >= SLOT * q + QUAD, row < SLOT * (q + 1))
        label_rows = jnp.where(spare, 0.0, label_rows)
    label_rows = label_rows.astype(BF)
    to_rows(cot, ct)
    cot_copies = start(0, owner_target, ct[...].astype(BF), label_rows, go=False)
    loads["w1"].wait()
    packed_one[...] = nn(normed, w1[...]).astype(BF)
    for load in ordered[8:]:
        load.start()
    pl.semaphore_wait(barrier, len(around))
    for copy in cot_copies:
        copy.start()
    loads["b1"].wait()

    def weight_one(score, h):
        t = score * SCALE + b1[h].astype(F32)
        return jnp.exp(t - jnp.max(t, axis=-1, keepdims=True))

    def weight_two(score, h):
        t = score * (SCALE * LOG2E) + table_two[h]
        return jnp.exp2(t - jnp.max(t, axis=-1, keepdims=True))

    attention(packed_one, weight_one, probs_one, heads_one, inv_one, masks)
    loads["wo1"].wait()
    mid_copies = start(1, owner_target, (x[...] + nn(heads_one[...], wo1[...])).astype(BF))

    for name in ("wup", "w2", "wo2", "fq"):
        loads[name].wait()
    for weight, turned in ((wup, wupt), (w2, w2t), (wo2, wo2t)):
        turned[...] = weight[...].T
    ct[...] = arrived(0, cot_copies)
    loads["wdn"].wait()
    dh_keep[...] = (0.5 * nt(ct[...].astype(BF), wdn[...])).astype(BF)
    label_rows = [first_recv[q, 9 + a] for q in range(4) for a in range(3)]
    label_here = nn(fq[...], jnp.concatenate(label_rows, axis=0))
    row = lax.broadcasted_iota(jnp.int32, (WT, LANES), 0)
    late_row = jnp.logical_or(
        jnp.logical_and(row >= PLANE // 2, row < PLANE), row >= PLANE + PLANE // 2
    )
    edge = jnp.where(i == 0, 1.0, 0.0).astype(F32)
    ids = label_here * 2.0 + jnp.where(late_row, edge, 0.0)
    lane = lax.broadcasted_iota(jnp.int32, (WT, LANES), 1).astype(F32)
    one_hot = jnp.where(ids == lane, 1.0, 0.0).astype(BF)
    barred = (nt(one_hot, one_hot) - 1.0) * 1e30
    loads["b2"].wait()
    for h in range(HEADS):
        table_two[h] = b2[h].astype(F32) * LOG2E + barred
    for name in ("g2", "g3"):
        loads[name].wait()

    mid = arrived(1, mid_copies)
    hat, rs_two = norm_parts(mid)
    hat_two[...] = hat
    packed_two[...] = nn((hat * g2[...]).astype(BF), w2[...]).astype(BF)
    attention(packed_two, weight_two, probs_two, heads_two, inv_two, masks)
    late = mid + nn(heads_two[...], wo2[...])

    hat, rs_three = norm_parts(late)
    normed = (hat * g3[...]).astype(BF)
    dn = feed_gradient(normed, wup, wupt, dh_keep, hidden).astype(BF).astype(F32)
    d_late = ct[...] + norm_back(hat, rs_three, g3[...], dn)

    d_heads[...] = nn(d_late.astype(BF), wo2t[...]).astype(BF)
    attention_back(packed_two, probs_two, heads_two, inv_two, d_heads, d_packed, masks)
    dn = nn(d_packed[...], w2t[...]).astype(BF).astype(F32)
    d_mid = d_late + norm_back(hat_two[...], rs_two, g2[...], dn)
    back_copies = start(2, window_target, d_mid.astype(BF))
    out_copies = start(3, window_target, (late + nn(hidden[...], wdn[...])).astype(BF))

    for weight, turned in ((wo1, wo1t), (w1, w1t)):
        turned[...] = weight[...].T

    d_mid = arrived(2, back_copies)
    d_heads[...] = nn(d_mid.astype(BF), wo1t[...]).astype(BF)
    attention_back(packed_one, probs_one, heads_one, inv_one, d_heads, d_packed, masks)
    to_cells(arrived(3, out_copies), outputs)
    dn = nn(d_packed[...], w1t[...]).astype(BF).astype(F32)
    to_cells(d_mid + norm_back(hat_one[...], rs_one, g1[...], dn), input_grad)
    for copy in cot_copies + mid_copies + back_copies + out_copies:
        copy.wait_send()


def write_out(first, second, first_out, second_out):
    first_out[...] = first[...]
    second_out[...] = second[...]


def per_device(n_lat, n_lon, *args):
    (tokens, labels, g1, w1, wo1, b1, g2, w2, wo2, b2, g3, wup, wdn, cot) = args
    place = quadrant_matrix()
    to_quad = jnp.asarray(place, BF)
    from_quad = jnp.asarray(place.T, BF)
    def cells(a):
        return a.transpose(1, 2, 0, 3).reshape(PLANE, LEV, D)

    operands = (
        cells(tokens), labels.transpose(1, 0, 2), g1.reshape(1, D), w1, wo1, b1, g2.reshape(1, D), w2, wo2, b2,
        g3.reshape(1, D), wup, wdn, cells(cot), to_quad, from_quad,
    )
    vm = pltpu.VMEM
    landing = [vm(a.shape, a.dtype) for a in operands]
    block = (PLANE, LEV, D)
    scratch = landing + [
        vm((WT, D), F32), vm((WT, D), F32),
        vm((WT, 3 * D), BF), vm((WT, 3 * D), BF),
        vm((HEADS * WT, WT), BF), vm((HEADS * WT, WT), BF),
        vm((WT, D), BF), vm((WT, D), BF), vm((WT, D), BF), vm((WT, 3 * D), BF),
        vm((WT, D), F32), vm((WT, D), F32), vm((WT, D), F32), vm((WT, D), F32),
        vm((WT, FF), BF), vm((WT, FF), BF), vm((HEADS, WT, WT), F32),
        vm((3 * D, D), BF), vm((D, D), BF), vm((3 * D, D), BF), vm((D, D), BF), vm((FF, D), BF),
        vm((4, 4, 9, TILE, LANES), BF), vm((4, 4, 9, TILE, LANES), BF),
        vm((4, 12, TILE, LANES), BF), vm((4, 12, TILE, LANES), BF),
        pltpu.SemaphoreType.DMA((len(operands),)),
        pltpu.SemaphoreType.DMA((4, 4)), pltpu.SemaphoreType.DMA((4, 4)),
    ]
    whole = pl.BlockSpec(memory_space=pl.ANY)
    results = pl.pallas_call(
        functools.partial(kernel, n_lat, n_lon),
        out_shape=(pltpu.VMEM(block, BF), pltpu.VMEM(block, BF)),
        in_specs=[whole] * len(operands),
        out_specs=[pl.BlockSpec(memory_space=pltpu.VMEM)] * 2,
        scratch_shapes=scratch,
        compiler_params=pltpu.CompilerParams(
            collective_id=0, has_side_effects=True, vmem_limit_bytes=56 * 1024 * 1024
        ),
    )(*operands)
    results = [pltpu.with_memory_space_constraint(a, pltpu.VMEM) for a in results]
    results = pl.pallas_call(
        write_out,
        out_shape=(jax.ShapeDtypeStruct(block, BF), jax.ShapeDtypeStruct(block, BF)),
        in_specs=[pl.BlockSpec(memory_space=pltpu.VMEM)] * 2,
        out_specs=[pl.BlockSpec(memory_space=pltpu.VMEM)] * 2,
    )(*results)
    return tuple(a.reshape(WLAT, WLON, LEV, D).transpose(2, 0, 1, 3) for a in results)


def solution(mesh):
    field = P(None, "lat", "lon", None)
    return jax.shard_map(
        functools.partial(per_device, mesh.shape["lat"], mesh.shape["lon"]),
        mesh=mesh,
        in_specs=(field, P(None, "lat", "lon")) + (P(),) * 11 + (field,),
        out_specs=(field, field),
        check_vma=False,
    )
```
